512 devices in a mesh: pipe: 16 (over z), seq: 32 (over x, y, core).
Axes of the slice: x: 4, y: 4, z: 16, core: 2. Of those that a mesh axis runs over, the one named last changes fastest.
Arguments:
- handoff: bfloat16 [16, 4096, 512], P('pipe', 'seq'), may hold values from -6 to 6
- gate_input: bfloat16 [16, 4096, 512], P('pipe', 'seq'), may hold values from -6 to 6
- source: bfloat16 [16, 4096, 512], P('pipe', 'seq'), may hold values from -6 to 6
- long_filter: bfloat16 [16, 4096, 512], P('pipe', 'seq'), may hold values from -6 to 6
- decay_rates: float32 [16, 512], P('pipe'), may hold values from 6.1035156e-05 to 0.0014648438
Outputs:
- grad_gate: bfloat16 [16, 4096, 512], P('pipe', 'seq')
- grad_source: bfloat16 [16, 4096, 512], P('pipe', 'seq')
- grad_filter: float32 [16, 4096, 512], P('pipe', 'seq')
The draws below stay inside these ranges and needn't reach their ends.
All inputs are finite; a program needn't handle non-finite values.
Results may differ from the reference program's by a relative error of at most 0.0049.
Values may be sent and summed in bfloat16 or wider, within the bound.
A program may use at most 64 MiB of HBM per device.

```python
import math
import jax
import jax.numpy as jnp
from jax import lax

D = 512
LEN = 4096
SECTIONS = 16


def block_scale(rng, shape, shards, least, largest):
    factor_of, own = 1.0, jax.random.fold_in(rng, 6)
    for axis_at, blocks in shards:
        heights = jnp.exp(jax.random.uniform(jax.random.fold_in(own, axis_at), (blocks,), jnp.float32, least / len(shards), largest / len(shards)))
        factor_of = factor_of * jnp.repeat(heights, shape[axis_at] // blocks).reshape([-1 if axis == axis_at else 1 for axis in range(len(shape))])
    return factor_of


def normal_values(own_key, dims, deviation, reach, shards=(), kind=jnp.bfloat16):
    level = block_scale(own_key, dims, shards, -0.22, 0.18) if shards else 1.0
    array = jax.random.normal(own_key, dims, jnp.float32) * deviation * level
    return jnp.minimum(jnp.maximum(array, -reach), reach).astype(kind)


def setup_inputs(seed: int = 0) -> dict:
    arg_keys = jax.random.split(jax.random.key(seed), 6)
    handoff = normal_values(arg_keys[0], (SECTIONS, LEN, D), 1.0, 6.0, ((0, 16), (1, 32)))
    gate_input = normal_values(arg_keys[1], (SECTIONS, LEN, D), 1.0, 6.0, ((0, 16), (1, 32)))
    source = normal_values(arg_keys[2], (SECTIONS, LEN, D), 1.0, 6.0, ((0, 16), (1, 32)))
    long_filter = normal_values(arg_keys[3], (SECTIONS, LEN, D), 1.0, 6.0, ((0, 16), (1, 32)))
    decay_rates = jnp.clip(jnp.exp(math.log(0.0014648438) - 3.1780538 * jax.random.uniform(arg_keys[4], (SECTIONS, D), jnp.float32) ** block_scale(arg_keys[4], (SECTIONS, D), ((0, 16),), -0.2, 0.2)), 6.103515625e-05, 0.0014648438)
    return {"handoff": handoff, "gate_input": gate_input, "source": source, "long_filter": long_filter, "decay_rates": decay_rates}


def one_section(items):
    grad_out, gate_input, source, long_filter, decay_rates = items
    steps_all = jnp.arange(LEN, dtype=jnp.float32)[:, None]
    modulation = jnp.sqrt(2.0 * decay_rates)[None, :] * jnp.exp(-decay_rates[None, :] * steps_all)
    kernel = long_filter.astype(jnp.float32) * modulation
    grad_conv = (grad_out.astype(jnp.float32) * gate_input.astype(jnp.float32)).astype(jnp.bfloat16)
    span_len = 2 * LEN
    spec_kernel = jnp.fft.rfft(kernel, n=span_len, axis=0)
    spec_source = jnp.fft.rfft(source.astype(jnp.float32), n=span_len, axis=0)
    spec_grad = jnp.fft.rfft(grad_conv.astype(jnp.float32), n=span_len, axis=0)
    conv = jnp.fft.irfft(spec_kernel * spec_source, n=span_len, axis=0)[:LEN]
    back = jnp.fft.irfft(jnp.conj(spec_kernel) * spec_grad, n=span_len, axis=0)[:LEN]
    grad_kernel = jnp.fft.irfft(jnp.conj(spec_source) * spec_grad, n=span_len, axis=0)[:LEN]
    grad_gate = (grad_out.astype(jnp.float32) * conv).astype(jnp.bfloat16)
    return (grad_gate, back.astype(jnp.bfloat16), (grad_kernel * modulation).astype(jnp.float32))

def reference(handoff, gate_input, source, long_filter, decay_rates):
    grad_out = jnp.roll(handoff, -1, axis=0)
    grad_gate, grad_source, grad_filter = lax.map(one_section, (grad_out, gate_input, source, long_filter, decay_rates))
    return (grad_gate, grad_source, grad_filter)
```

```python
import functools

import jax
import jax.numpy as jnp
import ml_dtypes
import numpy as np
from jax import lax
from jax.experimental import pallas as pl
from jax.experimental.pallas import tpu as pltpu
from jax.sharding import PartitionSpec as P

MESH = pl.DeviceIdType.MESH
F32, BF16 = jnp.float32, jnp.bfloat16
INNER = 512
TILE = 128
LANES = 128


def tables():
    token = np.arange(INNER, dtype=np.float64)[:, None]
    freq = np.arange(INNER, dtype=np.float64)[None, :] + 0.5
    angle = 2.0 * np.pi * ((token * freq) % (2 * INNER)) / (2 * INNER)
    forward = np.concatenate([np.cos(angle), -np.sin(angle)], axis=1)
    inverse = forward.T / INNER

    def split(table):
        high = table.astype(ml_dtypes.bfloat16)
        low = (table - high.astype(np.float64)).astype(ml_dtypes.bfloat16)
        return np.concatenate([high, low], axis=0)

    return split(forward), split(inverse)


def kernel(
    n,
    nz,
    handoff,
    gate,
    source,
    filt,
    decay,
    forward_hbm,
    inverse_hbm,
    out_gate,
    out_source,
    out_filter,
    src_v,
    gate_v,
    filt_v,
    decay_v,
    forward_v,
    inverse_v,
    grad_v,
    mod_v,
    send_in,
    recv_in,
    spec,
    prod,
    send_out,
    recv_out,
    og_v,
    os_v,
    of_v,
    local_sem,
    pipe_send,
    pipe_recv,
    in_send,
    in_recv,
    out_send,
    out_recv,
):
    me = lax.axis_index("seq")
    mz = lax.axis_index("pipe")
    above, below = lax.rem(mz + 1, nz), lax.rem(mz + nz - 1, nz)
    width = src_v.shape[1]
    chans = width // n
    chunks = width // LANES
    per_chunk = LANES // chans
    group = INNER // TILE
    blocks = n // group
    rows = blocks * chans

    loads = [
        pltpu.make_async_copy(source.at[0], src_v, local_sem.at[0]),
        pltpu.make_async_copy(filt.at[0], filt_v, local_sem.at[1]),
        pltpu.make_async_copy(decay, decay_v, local_sem.at[2]),
        pltpu.make_async_copy(gate.at[0], gate_v, local_sem.at[3]),
        pltpu.make_async_copy(forward_hbm, forward_v, local_sem.at[4]),
        pltpu.make_async_copy(inverse_hbm, inverse_v, local_sem.at[5]),
    ]
    for load in loads:
        load.start()

    barrier = pltpu.get_barrier_semaphore()

    def greet(i, carry):
        pl.semaphore_signal(
            barrier, inc=1, device_id={"seq": lax.rem(me + i, n)}, device_id_type=MESH
        )
        return carry

    pl.semaphore_signal(barrier, inc=1, device_id={"pipe": above}, device_id_type=MESH)
    lax.fori_loop(1, n, greet, 0)

    def by_channel(value):
        return value.astype(F32).T.astype(BF16).reshape(-1, chans, TILE)

    loads[0].wait()
    send_in[0] = by_channel(src_v[...])
    recv_in[0, me] = send_in[0, me]

    pl.semaphore_wait(barrier, n)

    def pipe_copy(q):
        at = pl.multiple_of(lax.rem(q + me, chunks) * LANES, LANES)
        return pltpu.make_async_remote_copy(
            src_ref=handoff.at[0, :, pl.ds(at, LANES)],
            dst_ref=grad_v.at[:, pl.ds(at, LANES)],
            send_sem=pipe_send.at[q],
            recv_sem=pipe_recv.at[q],
            device_id={"pipe": below},
            device_id_type=MESH,
        )

    for q in range(chunks):
        pipe_copy(q).start()

    def exchange(src, dst, which, send_sems, recv_sems, dest):
        pltpu.make_async_remote_copy(
            src_ref=src.at[which, dest],
            dst_ref=dst.at[which, me],
            send_sem=send_sems.at[which],
            recv_sem=recv_sems.at[which],
            device_id={"seq": dest},
            device_id_type=MESH,
        ).start()

    def whole(src, dst, which, send_sems, recv_sems):
        return pltpu.make_async_remote_copy(
            src_ref=src.at[which, pl.ds(0, n - 1)],
            dst_ref=dst.at[which, pl.ds(0, n - 1)],
            send_sem=send_sems.at[which],
            recv_sem=recv_sems.at[which],
            device_id={"seq": lax.rem(me + 1, n)},
            device_id_type=MESH,
        )

    def send_all(which):
        def step(i, carry):
            exchange(send_in, recv_in, which, in_send, in_recv, lax.rem(me + i, n))
            return carry

        lax.fori_loop(1, n, step, 0)

    send_all(0)

    loads[1].wait()
    loads[2].wait()
    rates = decay_v[...]
    steps = (lax.broadcasted_iota(jnp.int32, (TILE, width), 0) + me * TILE).astype(F32)
    mod_v[...] = jnp.sqrt(2.0 * rates) * jnp.exp(-rates * steps)
    send_in[1] = by_channel(filt_v[...].astype(F32) * mod_v[...])
    recv_in[1, me] = send_in[1, me]
    send_all(1)

    loads[3].wait()
    for q in range(chunks):
        pipe_copy(q).wait_recv()
        chunk = lax.rem(q + me, chunks)
        cols = pl.ds(pl.multiple_of(chunk * LANES, LANES), LANES)
        product = grad_v[:, cols].astype(F32) * gate_v[:, cols].astype(F32)
        send_in[2, pl.ds(chunk * per_chunk, per_chunk)] = by_channel(product.astype(BF16))

        def step(i, carry):
            dest = chunk * per_chunk + lax.rem(me + i, per_chunk)

            @pl.when(dest != me)
            def _():
                exchange(send_in, recv_in, 2, in_send, in_recv, dest)

            return carry

        lax.fori_loop(0, per_chunk, step, 0)
    recv_in[2, me] = send_in[2, me]

    def forward(which):
        block = recv_in[which].reshape(blocks, group, chans, TILE)
        left = jnp.concatenate([block[:, j] for j in range(group)], axis=-1).reshape(rows, INNER)
        for at in range(0, 2 * INNER, 256):
            spec[which, :, at : at + 256] = jnp.dot(
                left, forward_v[0:INNER, at : at + 256], preferred_element_type=F32
            ) + jnp.dot(
                left, forward_v[INNER : 2 * INNER, at : at + 256], preferred_element_type=F32
            )

    def multiply(kept, other, correlate):
        def step(g, carry):
            at = pl.multiple_of(g * LANES, LANES)
            real, imag = pl.ds(at, LANES), pl.ds(pl.multiple_of(at + INNER, LANES), LANES)
            lane = lax.broadcasted_iota(jnp.int32, (8, LANES), 1)
            sign = (1 - 2 * lax.rem(lane, 2)).astype(F32)
            for half in range(0, chans, 8):
                part = [pl.ds(b * chans + half, 8) for b in range(blocks)]
                raw = [(spec[kept, part[b], real], spec[kept, part[b], imag]) for b in range(blocks)]
                fold = [raw[0]]
                for b in range(1, blocks):
                    before = raw[b - 1]
                    fold.append((raw[b][0] - sign * before[1], raw[b][1] + sign * before[0]))
                right = [
                    (spec[other, part[b], real], spec[other, part[b], imag]) for b in range(blocks)
                ]
                for i in range(blocks):
                    total_r = total_i = None
                    for j in range(i, blocks) if correlate else range(i + 1):
                        kr, ki = fold[j - i] if correlate else fold[i - j]
                        br, bi = right[j]
                        if correlate:
                            term_r, term_i = kr * br + ki * bi, kr * bi - ki * br
                        else:
                            term_r, term_i = kr * br - ki * bi, kr * bi + ki * br
                        total_r = term_r if total_r is None else total_r + term_r
                        total_i = term_i if total_i is None else total_i + term_i
                    prod[part[i], real] = total_r
                    prod[part[i], imag] = total_i
            return carry

        lax.fori_loop(0, INNER // LANES, step, 0)

    def inverse(which):
        left = prod[...].astype(BF16)
        half = 2 * INNER
        for at in range(0, INNER, 256):
            result = jnp.dot(
                left, inverse_v[0:half, at : at + 256], preferred_element_type=F32
            ) + jnp.dot(left, inverse_v[half : 2 * half, at : at + 256], preferred_element_type=F32)
            result = result.astype(BF16)
            for j in range(256 // TILE):
                piece = result[:, j * TILE : (j + 1) * TILE].reshape(blocks, chans, TILE)
                for b in range(blocks):
                    send_out[which, b * group + at // TILE + j] = piece[b]
        recv_out[which, me] = send_out[which, me]

        def step(i, carry):
            exchange(send_out, recv_out, which, out_send, out_recv, lax.rem(me + i, n))
            return carry

        lax.fori_loop(1, n, step, 0)

    loads[4].wait()
    loads[5].wait()
    whole(send_in, recv_in, 0, in_send, in_recv).wait_recv()
    forward(0)
    whole(send_in, recv_in, 1, in_send, in_recv).wait_recv()
    forward(1)
    multiply(1, 0, False)
    inverse(0)
    whole(send_in, recv_in, 2, in_send, in_recv).wait_recv()
    forward(2)
    multiply(1, 2, True)
    inverse(1)
    multiply(0, 2, True)
    inverse(2)

    def by_token(which):
        return recv_out[which].reshape(width, TILE).astype(F32).T

    whole(send_out, recv_out, 0, out_send, out_recv).wait_recv()
    og_v[...] = (grad_v[...].astype(F32) * by_token(0)).astype(BF16)
    stores = [pltpu.make_async_copy(og_v, out_gate.at[0], local_sem.at[6])]
    stores[0].start()
    whole(send_out, recv_out, 1, out_send, out_recv).wait_recv()
    os_v[...] = by_token(1).astype(BF16)
    stores.append(pltpu.make_async_copy(os_v, out_source.at[0], local_sem.at[7]))
    stores[1].start()
    whole(send_out, recv_out, 2, out_send, out_recv).wait_recv()
    of_v[...] = by_token(2) * mod_v[...]
    stores.append(pltpu.make_async_copy(of_v, out_filter.at[0], local_sem.at[8]))
    stores[2].start()

    for q in range(chunks):
        pipe_copy(q).wait_send()
    for which in range(3):
        whole(send_in, recv_in, which, in_send, in_recv).wait_send()
        whole(send_out, recv_out, which, out_send, out_recv).wait_send()
    for store in stores:
        store.wait()


def local(n, nz, handoff, gate_input, source, long_filter, decay_rates):
    forward_table, inverse_table = tables()
    _, tokens, width = source.shape
    chans = width // n
    rows = n * TILE // INNER * chans
    block = (tokens, width)
    return pl.pallas_call(
        functools.partial(kernel, n, nz),
        out_shape=(
            jax.ShapeDtypeStruct(source.shape, BF16),
            jax.ShapeDtypeStruct(source.shape, BF16),
            jax.ShapeDtypeStruct(source.shape, F32),
        ),
        in_specs=[pl.BlockSpec(memory_space=pl.ANY)] * 7,
        out_specs=[pl.BlockSpec(memory_space=pl.ANY)] * 3,
        scratch_shapes=[
            pltpu.VMEM(block, BF16),
            pltpu.VMEM(block, BF16),
            pltpu.VMEM(block, BF16),
            pltpu.VMEM((1, width), F32),
            pltpu.VMEM(forward_table.shape, BF16),
            pltpu.VMEM(inverse_table.shape, BF16),
            pltpu.VMEM(block, BF16),
            pltpu.VMEM(block, F32),
            pltpu.VMEM((3, n, chans, TILE), BF16),
            pltpu.VMEM((3, n, chans, TILE), BF16),
            pltpu.VMEM((3, rows, 2 * INNER), F32),
            pltpu.VMEM((rows, 2 * INNER), F32),
            pltpu.VMEM((3, n, chans, TILE), BF16),
            pltpu.VMEM((3, n, chans, TILE), BF16),
            pltpu.VMEM(block, BF16),
            pltpu.VMEM(block, BF16),
            pltpu.VMEM(block, F32),
            pltpu.SemaphoreType.DMA((9,)),
            pltpu.SemaphoreType.DMA((width // LANES,)),
            pltpu.SemaphoreType.DMA((width // LANES,)),
            pltpu.SemaphoreType.DMA((3,)),
            pltpu.SemaphoreType.DMA((3,)),
            pltpu.SemaphoreType.DMA((3,)),
            pltpu.SemaphoreType.DMA((3,)),
        ],
        compiler_params=pltpu.CompilerParams(
            collective_id=0, has_side_effects=True, vmem_limit_bytes=60 * 1024 * 1024
        ),
        cost_estimate=pl.CostEstimate(
            flops=2 * 6 * rows * 4 * INNER * INNER, bytes_accessed=6 << 20, transcendentals=0
        ),
    )(
        handoff,
        gate_input,
        source,
        long_filter,
        decay_rates,
        jnp.asarray(forward_table),
        jnp.asarray(inverse_table),
    )


def solution(mesh):
    tokens = P("pipe", "seq", None)
    return jax.shard_map(
        functools.partial(local, mesh.shape["seq"], mesh.shape["pipe"]),
        mesh=mesh,
        in_specs=(tokens, tokens, tokens, tokens, P("pipe", None)),
        out_specs=(tokens, tokens, tokens),
        check_vma=False,
    )
```

```python
import functools

import jax
import jax.numpy as jnp
import ml_dtypes
import numpy as np
from jax import lax
from jax.experimental import pallas as pl
from jax.experimental.pallas import tpu as pltpu
from jax.sharding import PartitionSpec as P

MESH = pl.DeviceIdType.MESH
F32, BF16 = jnp.float32, jnp.bfloat16
INNER = 512
TILE = 128
LANES = 128


def tables():
    token = np.arange(INNER, dtype=np.float64)[:, None]
    freq = np.arange(INNER, dtype=np.float64)[None, :] + 0.5
    angle = 2.0 * np.pi * ((token * freq) % (2 * INNER)) / (2 * INNER)
    forward = np.concatenate([np.cos(angle), -np.sin(angle)], axis=1)
    inverse = forward.T / INNER

    def split(table):
        high = table.astype(ml_dtypes.bfloat16)
        low = (table - high.astype(np.float64)).astype(ml_dtypes.bfloat16)
        return np.concatenate([high, low], axis=0)

    return split(forward), split(inverse)


def kernel(
    n,
    nz,
    handoff,
    gate,
    source,
    filt,
    decay,
    forward_hbm,
    inverse_hbm,
    og_v,
    os_v,
    of_v,
    src_v,
    gate_v,
    filt_v,
    decay_v,
    forward_v,
    inverse_v,
    grad_v,
    mod_v,
    send_in,
    recv_in,
    spec,
    prod,
    send_out,
    recv_out,
    local_sem,
    pipe_ready,
    pipe_send,
    pipe_recv,
    in_send,
    in_recv,
    out_send,
    out_recv,
):
    me = lax.axis_index("seq")
    mz = lax.axis_index("pipe")
    above, below = lax.rem(mz + 1, nz), lax.rem(mz + nz - 1, nz)
    width = src_v.shape[1]
    chans = width // n
    chunks = width // LANES
    per_chunk = LANES // chans
    group = INNER // TILE
    blocks = n // group
    rows = blocks * chans

    loads = [
        pltpu.make_async_copy(source.at[0], src_v, local_sem.at[0]),
        pltpu.make_async_copy(filt.at[0], filt_v, local_sem.at[1]),
        pltpu.make_async_copy(decay, decay_v, local_sem.at[2]),
        pltpu.make_async_copy(gate.at[0], gate_v, local_sem.at[3]),
        pltpu.make_async_copy(forward_hbm, forward_v, local_sem.at[4]),
        pltpu.make_async_copy(inverse_hbm, inverse_v, local_sem.at[5]),
    ]
    for load in loads:
        load.start()

    barrier = pltpu.get_barrier_semaphore()

    def greet(i, carry):
        pl.semaphore_signal(
            barrier, inc=1, device_id={"seq": lax.rem(me + i, n)}, device_id_type=MESH
        )
        return carry

    first, last = mz == 0, mz == nz - 1

    @pl.when(jnp.logical_not(last))
    def _():
        pl.semaphore_signal(barrier, inc=1, device_id={"pipe": above}, device_id_type=MESH)

    @pl.when(first)
    def _():
        pl.semaphore_signal(barrier, inc=1, device_id={"pipe": below}, device_id_type=MESH)

    lax.fori_loop(1, n, greet, 0)

    def by_channel(value):
        return value.astype(F32).T.astype(BF16).reshape(-1, chans, TILE)

    loads[0].wait()
    send_in[0] = by_channel(src_v[...])
    recv_in[0, me] = send_in[0, me]

    pl.semaphore_wait(barrier, n - 1 + jnp.where(first, 0, 1) + jnp.where(last, 1, 0))

    def pipe_copy(q):
        at = pl.multiple_of(lax.rem(q + me, chunks) * LANES, LANES)
        return pltpu.make_async_remote_copy(
            src_ref=handoff.at[0, :, pl.ds(at, LANES)],
            dst_ref=grad_v.at[:, pl.ds(at, LANES)],
            send_sem=pipe_send.at[q],
            recv_sem=pipe_recv.at[q],
            device_id={"pipe": below},
            device_id_type=MESH,
        )

    def pass_on():
        for q in range(chunks):
            pipe_copy(q).start()

    pl.when(jnp.logical_not(first))(pass_on)

    @pl.when(last)
    def _():
        pl.semaphore_signal(pipe_ready, inc=1, device_id={"pipe": above}, device_id_type=MESH)

    def exchange(src, dst, which, send_sems, recv_sems, dest):
        pltpu.make_async_remote_copy(
            src_ref=src.at[which, dest],
            dst_ref=dst.at[which, me],
            send_sem=send_sems.at[which],
            recv_sem=recv_sems.at[which],
            device_id={"seq": dest},
            device_id_type=MESH,
        ).start()

    def whole(src, dst, which, send_sems, recv_sems):
        return pltpu.make_async_remote_copy(
            src_ref=src.at[which, pl.ds(0, n - 1)],
            dst_ref=dst.at[which, pl.ds(0, n - 1)],
            send_sem=send_sems.at[which],
            recv_sem=recv_sems.at[which],
            device_id={"seq": lax.rem(me + 1, n)},
            device_id_type=MESH,
        )

    def send_all(which):
        def step(i, carry):
            exchange(send_in, recv_in, which, in_send, in_recv, lax.rem(me + i, n))
            return carry

        lax.fori_loop(1, n, step, 0)

    send_all(0)

    loads[1].wait()
    loads[2].wait()
    rates = decay_v[...]
    steps = (lax.broadcasted_iota(jnp.int32, (TILE, width), 0) + me * TILE).astype(F32)
    mod_v[...] = jnp.sqrt(2.0 * rates) * jnp.exp(-rates * steps)
    send_in[1] = by_channel(filt_v[...].astype(F32) * mod_v[...])
    recv_in[1, me] = send_in[1, me]
    send_all(1)

    loads[3].wait()
    for q in range(chunks):
        pipe_copy(q).wait_recv()
        chunk = lax.rem(q + me, chunks)
        cols = pl.ds(pl.multiple_of(chunk * LANES, LANES), LANES)
        product = grad_v[:, cols].astype(F32) * gate_v[:, cols].astype(F32)
        send_in[2, pl.ds(chunk * per_chunk, per_chunk)] = by_channel(product.astype(BF16))

        def step(i, carry):
            dest = chunk * per_chunk + lax.rem(me + i, per_chunk)

            @pl.when(dest != me)
            def _():
                exchange(send_in, recv_in, 2, in_send, in_recv, dest)

            return carry

        lax.fori_loop(0, per_chunk, step, 0)
    recv_in[2, me] = send_in[2, me]

    @pl.when(first)
    def _():
        pl.semaphore_wait(pipe_ready, 1)
        pass_on()


    def forward(which):
        block = recv_in[which].reshape(blocks, group, chans, TILE)
        left = jnp.concatenate([block[:, j] for j in range(group)], axis=-1).reshape(rows, INNER)
        for at in range(0, 2 * INNER, 256):
            spec[which, :, at : at + 256] = jnp.dot(
                left, forward_v[0:INNER, at : at + 256], preferred_element_type=F32
            ) + jnp.dot(
                left, forward_v[INNER : 2 * INNER, at : at + 256], preferred_element_type=F32
            )

    def multiply(kept, other, correlate):
        def step(g, carry):
            at = pl.multiple_of(g * LANES, LANES)
            real, imag = pl.ds(at, LANES), pl.ds(pl.multiple_of(at + INNER, LANES), LANES)
            lane = lax.broadcasted_iota(jnp.int32, (8, LANES), 1)
            sign = (1 - 2 * lax.rem(lane, 2)).astype(F32)
            for half in range(0, chans, 8):
                part = [pl.ds(b * chans + half, 8) for b in range(blocks)]
                raw = [(spec[kept, part[b], real], spec[kept, part[b], imag]) for b in range(blocks)]
                fold = [raw[0]]
                for b in range(1, blocks):
                    before = raw[b - 1]
                    fold.append((raw[b][0] - sign * before[1], raw[b][1] + sign * before[0]))
                right = [
                    (spec[other, part[b], real], spec[other, part[b], imag]) for b in range(blocks)
                ]
                for i in range(blocks):
                    total_r = total_i = None
                    for j in range(i, blocks) if correlate else range(i + 1):
                        kr, ki = fold[j - i] if correlate else fold[i - j]
                        br, bi = right[j]
                        if correlate:
                            term_r, term_i = kr * br + ki * bi, kr * bi - ki * br
                        else:
                            term_r, term_i = kr * br - ki * bi, kr * bi + ki * br
                        total_r = term_r if total_r is None else total_r + term_r
                        total_i = term_i if total_i is None else total_i + term_i
                    prod[part[i], real] = total_r
                    prod[part[i], imag] = total_i
            return carry

        lax.fori_loop(0, INNER // LANES, step, 0)

    def inverse(which):
        left = prod[...].astype(BF16)
        half = 2 * INNER
        for at in range(0, INNER, 256):
            result = jnp.dot(
                left, inverse_v[0:half, at : at + 256], preferred_element_type=F32
            ) + jnp.dot(left, inverse_v[half : 2 * half, at : at + 256], preferred_element_type=F32)
            result = result.astype(BF16)
            for j in range(256 // TILE):
                piece = result[:, j * TILE : (j + 1) * TILE].reshape(blocks, chans, TILE)
                for b in range(blocks):
                    send_out[which, b * group + at // TILE + j] = piece[b]
        recv_out[which, me] = send_out[which, me]

        def step(i, carry):
            exchange(send_out, recv_out, which, out_send, out_recv, lax.rem(me + i, n))
            return carry

        lax.fori_loop(1, n, step, 0)

    loads[4].wait()
    loads[5].wait()
    whole(send_in, recv_in, 0, in_send, in_recv).wait_recv()
    forward(0)
    whole(send_in, recv_in, 1, in_send, in_recv).wait_recv()
    forward(1)
    multiply(1, 0, False)
    inverse(0)
    whole(send_in, recv_in, 2, in_send, in_recv).wait_recv()
    forward(2)
    multiply(1, 2, True)
    inverse(1)
    multiply(0, 2, True)
    inverse(2)

    def by_token(which):
        return recv_out[which].reshape(width, TILE).astype(F32).T

    whole(send_out, recv_out, 0, out_send, out_recv).wait_recv()
    og_v[...] = (grad_v[...].astype(F32) * by_token(0)).astype(BF16)
    whole(send_out, recv_out, 1, out_send, out_recv).wait_recv()
    os_v[...] = by_token(1).astype(BF16)
    whole(send_out, recv_out, 2, out_send, out_recv).wait_recv()
    of_v[...] = by_token(2) * mod_v[...]

    for q in range(chunks):
        pipe_copy(q).wait_send()
    for which in range(3):
        whole(send_in, recv_in, which, in_send, in_recv).wait_send()
        whole(send_out, recv_out, which, out_send, out_recv).wait_send()


def write_out(gate_v, source_v, filter_v, out_gate, out_source, out_filter, sems):
    stores = [
        pltpu.make_async_copy(filter_v, out_filter.at[0], sems.at[0]),
        pltpu.make_async_copy(source_v, out_source.at[0], sems.at[1]),
        pltpu.make_async_copy(gate_v, out_gate.at[0], sems.at[2]),
    ]
    for store in stores:
        store.start()
    for store in stores:
        store.wait()


def local(n, nz, handoff, gate_input, source, long_filter, decay_rates):
    forward_table, inverse_table = tables()
    _, tokens, width = source.shape
    chans = width // n
    rows = n * TILE // INNER * chans
    block = (tokens, width)
    hbm = lambda value: pltpu.with_memory_space_constraint(value, pltpu.HBM)
    results = pl.pallas_call(
        functools.partial(kernel, n, nz),
        out_shape=(
            pltpu.VMEM(block, BF16),
            pltpu.VMEM(block, BF16),
            pltpu.VMEM(block, F32),
        ),
        in_specs=[pl.BlockSpec(memory_space=pltpu.HBM)] * 7,
        out_specs=[pl.BlockSpec(memory_space=pltpu.VMEM)] * 3,
        scratch_shapes=[
            pltpu.VMEM(block, BF16),
            pltpu.VMEM(block, BF16),
            pltpu.VMEM(block, BF16),
            pltpu.VMEM((1, width), F32),
            pltpu.VMEM(forward_table.shape, BF16),
            pltpu.VMEM(inverse_table.shape, BF16),
            pltpu.VMEM(block, BF16),
            pltpu.VMEM(block, F32),
            pltpu.VMEM((3, n, chans, TILE), BF16),
            pltpu.VMEM((3, n, chans, TILE), BF16),
            pltpu.VMEM((3, rows, 2 * INNER), F32),
            pltpu.VMEM((rows, 2 * INNER), F32),
            pltpu.VMEM((3, n, chans, TILE), BF16),
            pltpu.VMEM((3, n, chans, TILE), BF16),
            pltpu.SemaphoreType.DMA((6,)),
            pltpu.SemaphoreType.REGULAR,
            pltpu.SemaphoreType.DMA((width // LANES,)),
            pltpu.SemaphoreType.DMA((width // LANES,)),
            pltpu.SemaphoreType.DMA((3,)),
            pltpu.SemaphoreType.DMA((3,)),
            pltpu.SemaphoreType.DMA((3,)),
            pltpu.SemaphoreType.DMA((3,)),
        ],
        compiler_params=pltpu.CompilerParams(
            collective_id=0, has_side_effects=True, vmem_limit_bytes=40 * 1024 * 1024
        ),
        cost_estimate=pl.CostEstimate(
            flops=2 * 6 * rows * 4 * INNER * INNER, bytes_accessed=6 << 20, transcendentals=0
        ),
    )(
        hbm(handoff),
        hbm(gate_input),
        hbm(source),
        hbm(long_filter),
        hbm(decay_rates),
        hbm(jnp.asarray(forward_table)),
        hbm(jnp.asarray(inverse_table)),
    )
    return pl.pallas_call(
        write_out,
        out_shape=tuple(jax.ShapeDtypeStruct(source.shape, r.dtype) for r in results),
        in_specs=[pl.BlockSpec(memory_space=pltpu.VMEM)] * 3,
        out_specs=[pl.BlockSpec(memory_space=pltpu.HBM)] * 3,
        scratch_shapes=[pltpu.SemaphoreType.DMA((3,))],
        compiler_params=pltpu.CompilerParams(vmem_limit_bytes=4 * 1024 * 1024),
    )(*[pltpu.with_memory_space_constraint(r, pltpu.VMEM) for r in results])


def solution(mesh):
    tokens = P("pipe", "seq", None)
    return jax.shard_map(
        functools.partial(local, mesh.shape["seq"], mesh.shape["pipe"]),
        mesh=mesh,
        in_specs=(tokens, tokens, tokens, tokens, P("pipe", None)),
        out_specs=(tokens, tokens, tokens),
        check_vma=False,
    )
```

```python
import functools

import jax
import jax.numpy as jnp
import ml_dtypes
import numpy as np
from jax import lax
from jax.experimental import pallas as pl
from jax.experimental.pallas import tpu as pltpu
from jax.sharding import PartitionSpec as P

MESH = pl.DeviceIdType.MESH
F32, BF16 = jnp.float32, jnp.bfloat16
INNER = 512
TILE = 128
LANES = 128


def tables():
    token = np.arange(INNER, dtype=np.float64)[:, None]
    freq = np.arange(INNER, dtype=np.float64)[None, :] + 0.5
    angle = 2.0 * np.pi * ((token * freq) % (2 * INNER)) / (2 * INNER)
    forward = np.concatenate([np.cos(angle), -np.sin(angle)], axis=1)
    inverse = forward.T / INNER

    def split(table):
        high = table.astype(ml_dtypes.bfloat16)
        low = (table - high.astype(np.float64)).astype(ml_dtypes.bfloat16)
        return np.concatenate([high, low], axis=0)

    return split(forward), split(inverse)


def kernel(
    n,
    nz,
    handoff,
    gate,
    source,
    filt,
    decay,
    forward_hbm,
    inverse_hbm,
    og_v,
    os_v,
    of_v,
    src_v,
    gate_v,
    filt_v,
    decay_v,
    forward_v,
    inverse_v,
    grad_v,
    mod_v,
    send_in,
    recv_in,
    spec,
    prod,
    send_out,
    recv_out,
    local_sem,
    pipe_ready,
    pipe_send,
    pipe_recv,
    in_send,
    in_recv,
    out_send,
    out_recv,
):
    me = lax.axis_index("seq")
    mz = lax.axis_index("pipe")
    above, below = lax.rem(mz + 1, nz), lax.rem(mz + nz - 1, nz)
    width = src_v.shape[1]
    chans = width // n
    chunks = width // LANES
    per_chunk = LANES // chans
    group = INNER // TILE
    blocks = n // group
    rows = blocks * chans

    nx, ny, nc = n // 8, 4, 2
    xs = [lax.rem(me // 8 + d, nx) for d in range(nx)]
    ys = [lax.rem(lax.rem(me // nc, ny) + d, ny) for d in range(ny)]
    cs = [lax.rem(lax.rem(me, nc) + d, nc) for d in range(nc)]

    def hops(offset):
        dx, dy, dc = offset
        return min(dx, nx - dx) + min(dy, ny - dy) + 0.1 * dc

    def index(offset):
        dx, dy, dc = offset
        return xs[dx] * (ny * nc) + ys[dy] * nc + cs[dc]

    offsets = [(dx, dy, dc) for dx in range(nx) for dy in range(ny) for dc in range(nc)]
    offsets = sorted(offsets, key=hops, reverse=True)[:-1]
    turns = sorted(range(nx), key=lambda d: min(d, nx - d), reverse=True)

    barrier = pltpu.get_barrier_semaphore()

    for offset in offsets:
        pl.semaphore_signal(barrier, inc=1, device_id={"seq": index(offset)}, device_id_type=MESH)

    first, last = mz == 0, mz == nz - 1

    @pl.when(jnp.logical_not(last))
    def _():
        pl.semaphore_signal(barrier, inc=1, device_id={"pipe": above}, device_id_type=MESH)

    @pl.when(first)
    def _():
        pl.semaphore_signal(barrier, inc=1, device_id={"pipe": below}, device_id_type=MESH)


    loads = [
        pltpu.make_async_copy(source.at[0], src_v, local_sem.at[0]),
        pltpu.make_async_copy(filt.at[0], filt_v, local_sem.at[1]),
        pltpu.make_async_copy(decay, decay_v, local_sem.at[2]),
        pltpu.make_async_copy(gate.at[0], gate_v, local_sem.at[3]),
        pltpu.make_async_copy(forward_hbm, forward_v, local_sem.at[4]),
        pltpu.make_async_copy(inverse_hbm, inverse_v, local_sem.at[5]),
    ]
    for load in loads:
        load.start()

    def by_channel(value):
        return value.astype(F32).T.astype(BF16).reshape(-1, chans, TILE)

    loads[0].wait()
    send_in[0] = by_channel(src_v[...])
    recv_in[0, me] = send_in[0, me]

    pl.semaphore_wait(barrier, n - 1 + jnp.where(first, 0, 1) + jnp.where(last, 1, 0))

    def pipe_copy(q):
        at = pl.multiple_of(xs[turns[q]] * LANES, LANES)
        return pltpu.make_async_remote_copy(
            src_ref=handoff.at[0, :, pl.ds(at, LANES)],
            dst_ref=grad_v.at[:, pl.ds(at, LANES)],
            send_sem=pipe_send.at[q],
            recv_sem=pipe_recv.at[q],
            device_id={"pipe": below},
            device_id_type=MESH,
        )

    def pass_on():
        for q in range(chunks):
            pipe_copy(q).start()

    pl.when(jnp.logical_not(first))(pass_on)

    @pl.when(last)
    def _():
        pl.semaphore_signal(pipe_ready, inc=1, device_id={"pipe": above}, device_id_type=MESH)

    def exchange(src, dst, which, send_sems, recv_sems, dest):
        pltpu.make_async_remote_copy(
            src_ref=src.at[which, dest],
            dst_ref=dst.at[which, me],
            send_sem=send_sems.at[which],
            recv_sem=recv_sems.at[which],
            device_id={"seq": dest},
            device_id_type=MESH,
        ).start()

    def whole(src, dst, which, send_sems, recv_sems):
        return pltpu.make_async_remote_copy(
            src_ref=src.at[which, pl.ds(0, n - 1)],
            dst_ref=dst.at[which, pl.ds(0, n - 1)],
            send_sem=send_sems.at[which],
            recv_sem=recv_sems.at[which],
            device_id={"seq": lax.rem(me + 1, n)},
            device_id_type=MESH,
        )

    def send_all(which):
        for offset in offsets:
            exchange(send_in, recv_in, which, in_send, in_recv, index(offset))

    send_all(0)

    loads[1].wait()
    loads[2].wait()
    rates = decay_v[...]
    steps = (lax.broadcasted_iota(jnp.int32, (TILE, width), 0) + me * TILE).astype(F32)
    mod_v[...] = jnp.sqrt(2.0 * rates) * jnp.exp(-rates * steps)
    send_in[1] = by_channel(filt_v[...].astype(F32) * mod_v[...])
    recv_in[1, me] = send_in[1, me]
    send_all(1)

    loads[3].wait()
    for q in range(chunks):
        pipe_copy(q).wait_recv()
        chunk = xs[turns[q]]
        cols = pl.ds(pl.multiple_of(chunk * LANES, LANES), LANES)
        product = grad_v[:, cols].astype(F32) * gate_v[:, cols].astype(F32)
        send_in[2, pl.ds(chunk * per_chunk, per_chunk)] = by_channel(product.astype(BF16))

        for offset in offsets:
            if offset[0] == turns[q]:
                exchange(send_in, recv_in, 2, in_send, in_recv, index(offset))
    recv_in[2, me] = send_in[2, me]

    @pl.when(first)
    def _():
        pl.semaphore_wait(pipe_ready, 1)
        pass_on()


    def forward(which):
        block = recv_in[which].reshape(blocks, group, chans, TILE)
        left = jnp.concatenate([block[:, j] for j in range(group)], axis=-1).reshape(rows, INNER)
        for at in range(0, 2 * INNER, 256):
            spec[which, :, at : at + 256] = jnp.dot(
                left, forward_v[0:INNER, at : at + 256], preferred_element_type=F32
            ) + jnp.dot(
                left, forward_v[INNER : 2 * INNER, at : at + 256], preferred_element_type=F32
            )

    def multiply(kept, other, correlate):
        def step(g, carry):
            at = pl.multiple_of(g * LANES, LANES)
            real, imag = pl.ds(at, LANES), pl.ds(pl.multiple_of(at + INNER, LANES), LANES)
            lane = lax.broadcasted_iota(jnp.int32, (8, LANES), 1)
            sign = (1 - 2 * lax.rem(lane, 2)).astype(F32)
            for half in range(0, chans, 8):
                part = [pl.ds(b * chans + half, 8) for b in range(blocks)]
                raw = [(spec[kept, part[b], real], spec[kept, part[b], imag]) for b in range(blocks)]
                fold = [raw[0]]
                for b in range(1, blocks):
                    before = raw[b - 1]
                    fold.append((raw[b][0] - sign * before[1], raw[b][1] + sign * before[0]))
                right = [
                    (spec[other, part[b], real], spec[other, part[b], imag]) for b in range(blocks)
                ]
                for i in range(blocks):
                    total_r = total_i = None
                    for j in range(i, blocks) if correlate else range(i + 1):
                        kr, ki = fold[j - i] if correlate else fold[i - j]
                        br, bi = right[j]
                        if correlate:
                            term_r, term_i = kr * br + ki * bi, kr * bi - ki * br
                        else:
                            term_r, term_i = kr * br - ki * bi, kr * bi + ki * br
                        total_r = term_r if total_r is None else total_r + term_r
                        total_i = term_i if total_i is None else total_i + term_i
                    prod[part[i], real] = total_r
                    prod[part[i], imag] = total_i
            return carry

        lax.fori_loop(0, INNER // LANES, step, 0)

    def inverse(which):
        left = prod[...].astype(BF16)
        half = 2 * INNER
        for at in range(0, INNER, 256):
            result = jnp.dot(
                left, inverse_v[0:half, at : at + 256], preferred_element_type=F32
            ) + jnp.dot(left, inverse_v[half : 2 * half, at : at + 256], preferred_element_type=F32)
            result = result.astype(BF16)
            for j in range(256 // TILE):
                piece = result[:, j * TILE : (j + 1) * TILE].reshape(blocks, chans, TILE)
                for b in range(blocks):
                    send_out[which, b * group + at // TILE + j] = piece[b]
        recv_out[which, me] = send_out[which, me]

        for offset in offsets:
            exchange(send_out, recv_out, which, out_send, out_recv, index(offset))

    loads[4].wait()
    loads[5].wait()
    whole(send_in, recv_in, 0, in_send, in_recv).wait_recv()
    forward(0)
    whole(send_in, recv_in, 1, in_send, in_recv).wait_recv()
    forward(1)
    multiply(1, 0, False)
    inverse(0)
    whole(send_in, recv_in, 2, in_send, in_recv).wait_recv()
    forward(2)
    multiply(1, 2, True)
    inverse(1)
    multiply(0, 2, True)
    inverse(2)

    def by_token(which):
        return recv_out[which].reshape(width, TILE).astype(F32).T

    whole(send_out, recv_out, 0, out_send, out_recv).wait_recv()
    og_v[...] = (grad_v[...].astype(F32) * by_token(0)).astype(BF16)
    whole(send_out, recv_out, 1, out_send, out_recv).wait_recv()
    os_v[...] = by_token(1).astype(BF16)
    whole(send_out, recv_out, 2, out_send, out_recv).wait_recv()
    of_v[...] = by_token(2) * mod_v[...]

    for q in range(chunks):
        pipe_copy(q).wait_send()
    for which in range(3):
        whole(send_in, recv_in, which, in_send, in_recv).wait_send()
        whole(send_out, recv_out, which, out_send, out_recv).wait_send()


def write_out(gate_v, source_v, filter_v, out_gate, out_source, out_filter, sems):
    stores = [
        pltpu.make_async_copy(filter_v, out_filter.at[0], sems.at[0]),
        pltpu.make_async_copy(source_v, out_source.at[0], sems.at[1]),
        pltpu.make_async_copy(gate_v, out_gate.at[0], sems.at[2]),
    ]
    for store in stores:
        store.start()
    for store in stores:
        store.wait()


def local(n, nz, handoff, gate_input, source, long_filter, decay_rates):
    forward_table, inverse_table = tables()
    _, tokens, width = source.shape
    chans = width // n
    rows = n * TILE // INNER * chans
    block = (tokens, width)
    hbm = lambda value: pltpu.with_memory_space_constraint(value, pltpu.HBM)
    results = pl.pallas_call(
        functools.partial(kernel, n, nz),
        out_shape=(
            pltpu.VMEM(block, BF16),
            pltpu.VMEM(block, BF16),
            pltpu.VMEM(block, F32),
        ),
        in_specs=[pl.BlockSpec(memory_space=pltpu.HBM)] * 7,
        out_specs=[pl.BlockSpec(memory_space=pltpu.VMEM)] * 3,
        scratch_shapes=[
            pltpu.VMEM(block, BF16),
            pltpu.VMEM(block, BF16),
            pltpu.VMEM(block, BF16),
            pltpu.VMEM((1, width), F32),
            pltpu.VMEM(forward_table.shape, BF16),
            pltpu.VMEM(inverse_table.shape, BF16),
            pltpu.VMEM(block, BF16),
            pltpu.VMEM(block, F32),
            pltpu.VMEM((3, n, chans, TILE), BF16),
            pltpu.VMEM((3, n, chans, TILE), BF16),
            pltpu.VMEM((3, rows, 2 * INNER), F32),
            pltpu.VMEM((rows, 2 * INNER), F32),
            pltpu.VMEM((3, n, chans, TILE), BF16),
            pltpu.VMEM((3, n, chans, TILE), BF16),
            pltpu.SemaphoreType.DMA((6,)),
            pltpu.SemaphoreType.REGULAR,
            pltpu.SemaphoreType.DMA((width // LANES,)),
            pltpu.SemaphoreType.DMA((width // LANES,)),
            pltpu.SemaphoreType.DMA((3,)),
            pltpu.SemaphoreType.DMA((3,)),
            pltpu.SemaphoreType.DMA((3,)),
            pltpu.SemaphoreType.DMA((3,)),
        ],
        compiler_params=pltpu.CompilerParams(
            collective_id=0, has_side_effects=True, vmem_limit_bytes=40 * 1024 * 1024
        ),
        cost_estimate=pl.CostEstimate(
            flops=2 * 6 * rows * 4 * INNER * INNER, bytes_accessed=6 << 20, transcendentals=0
        ),
    )(
        hbm(handoff),
        hbm(gate_input),
        hbm(source),
        hbm(long_filter),
        hbm(decay_rates),
        hbm(jnp.asarray(forward_table)),
        hbm(jnp.asarray(inverse_table)),
    )
    return pl.pallas_call(
        write_out,
        out_shape=tuple(jax.ShapeDtypeStruct(source.shape, r.dtype) for r in results),
        in_specs=[pl.BlockSpec(memory_space=pltpu.VMEM)] * 3,
        out_specs=[pl.BlockSpec(memory_space=pltpu.HBM)] * 3,
        scratch_shapes=[pltpu.SemaphoreType.DMA((3,))],
        compiler_params=pltpu.CompilerParams(vmem_limit_bytes=4 * 1024 * 1024),
    )(*[pltpu.with_memory_space_constraint(r, pltpu.VMEM) for r in results])


def solution(mesh):
    tokens = P("pipe", "seq", None)
    return jax.shard_map(
        functools.partial(local, mesh.shape["seq"], mesh.shape["pipe"]),
        mesh=mesh,
        in_specs=(tokens, tokens, tokens, tokens, P("pipe", None)),
        out_specs=(tokens, tokens, tokens),
        check_vma=False,
    )
```

```python
import functools

import jax
import jax.numpy as jnp
import ml_dtypes
import numpy as np
from jax import lax
from jax.experimental import pallas as pl
from jax.experimental.pallas import tpu as pltpu
from jax.sharding import PartitionSpec as P

MESH = pl.DeviceIdType.MESH
F32, BF16 = jnp.float32, jnp.bfloat16
INNER = 512
TILE = 128
LANES = 128
SOURCE, KERNEL, GRAD = 0, 1, 2


def tables():
    token = np.arange(INNER, dtype=np.float64)[:, None]
    freq = np.arange(INNER, dtype=np.float64)[None, :] + 0.5
    angle = 2.0 * np.pi * ((token * freq) % (2 * INNER)) / (2 * INNER)
    forward = np.concatenate([np.cos(angle), -np.sin(angle)], axis=1)
    inverse = forward.T / INNER

    def split(table):
        high = table.astype(ml_dtypes.bfloat16)
        low = (table - high.astype(np.float64)).astype(ml_dtypes.bfloat16)
        return np.concatenate([high, low], axis=0)

    return split(forward), split(inverse)


def kernel(
    n,
    nz,
    handoff,
    gate,
    source,
    filt,
    decay,
    forward_hbm,
    inverse_hbm,
    og_v,
    pair_v,
    mod_v,
    src_v,
    gate_v,
    filt_v,
    decay_v,
    forward_v,
    inverse_v,
    grad_v,
    send_first,
    recv_first,
    send_grad,
    recv_grad,
    spec,
    prod,
    send_conv,
    recv_conv,
    send_pair,
    local_sem,
    pipe_ready,
    all_in,
    pipe_send,
    pipe_recv,
    send_sem,
    recv_sem,
):
    me = lax.axis_index("seq")
    mz = lax.axis_index("pipe")
    above, below = lax.rem(mz + 1, nz), lax.rem(mz + nz - 1, nz)
    width = src_v.shape[1]
    chans = width // n
    chunks = width // LANES
    per_chunk = LANES // chans
    group = INNER // TILE
    blocks = n // group
    rows = blocks * chans

    nx, ny, nc = n // 8, 4, 2
    xs = [lax.rem(me // 8 + d, nx) for d in range(nx)]
    ys = [lax.rem(lax.rem(me // nc, ny) + d, ny) for d in range(ny)]
    cs = [lax.rem(lax.rem(me, nc) + d, nc) for d in range(nc)]

    def hops(offset):
        dx, dy, dc = offset
        return min(dx, nx - dx) + min(dy, ny - dy) + 0.1 * dc

    def index(offset):
        dx, dy, dc = offset
        return xs[dx] * (ny * nc) + ys[dy] * nc + cs[dc]

    offsets = [(dx, dy, dc) for dx in range(nx) for dy in range(ny) for dc in range(nc)]
    offsets = sorted(offsets, key=hops, reverse=True)[:-1]
    turns = sorted(range(nx), key=lambda d: min(d, nx - d), reverse=True)

    core = lax.rem(me, nc)
    second = me - core + 1
    sibling = me + 1 - 2 * core
    first, last = mz == 0, mz == nz - 1
    barrier = pltpu.get_barrier_semaphore()

    @pl.when(jnp.logical_not(last))
    def _():
        pl.semaphore_signal(
            barrier, inc=1, device_id={"pipe": above, "seq": second}, device_id_type=MESH
        )

    pl.semaphore_signal(barrier, inc=1, device_id={"seq": sibling}, device_id_type=MESH)
    for dx, dy, dc in offsets:
        if dc == 0:
            at = xs[dx] * (ny * nc) + ys[dy] * nc
            pl.semaphore_signal(barrier, inc=1, device_id={"seq": at}, device_id_type=MESH)

    @pl.when(first)
    def _():
        pl.semaphore_signal(
            barrier, inc=1, device_id={"pipe": below, "seq": second}, device_id_type=MESH
        )

    loads = [
        pltpu.make_async_copy(source.at[0], src_v, local_sem.at[0]),
        pltpu.make_async_copy(filt.at[0], filt_v, local_sem.at[1]),
        pltpu.make_async_copy(decay, decay_v, local_sem.at[2]),
        pltpu.make_async_copy(gate.at[0], gate_v, local_sem.at[3]),
        pltpu.make_async_copy(forward_hbm, forward_v, local_sem.at[4]),
        pltpu.make_async_copy(inverse_hbm, inverse_v, local_sem.at[5]),
    ]
    for load in loads:
        load.start()

    def pipe_copy(q):
        at = pl.multiple_of(xs[turns[q]] * LANES, LANES)
        return pltpu.make_async_remote_copy(
            src_ref=handoff.at[0, :, pl.ds(at, LANES)],
            dst_ref=grad_v.at[:, pl.ds(at, LANES)],
            send_sem=pipe_send.at[q],
            recv_sem=pipe_recv.at[q],
            device_id={"pipe": below},
            device_id_type=MESH,
        )

    def pass_on():
        for q in range(chunks):
            pipe_copy(q).start()

    @pl.when(core == 1)
    def _():
        pl.semaphore_wait(barrier, 1 + jnp.where(first, 0, 2) + jnp.where(last, 2, 0))

        @pl.when(jnp.logical_not(first))
        def _():
            pl.semaphore_signal(pipe_ready, inc=1, device_id={"seq": sibling}, device_id_type=MESH)
            pass_on()

        @pl.when(last)
        def _():
            for to in (second - 1, second):
                pl.semaphore_signal(
                    pipe_ready, inc=1, device_id={"pipe": above, "seq": to}, device_id_type=MESH
                )

    @pl.when(jnp.logical_and(core == 0, jnp.logical_not(first)))
    def _():
        pl.semaphore_wait(pipe_ready, 1)
        pass_on()

    def by_channel(value):
        return value.astype(F32).T.astype(BF16).reshape(-1, chans, TILE)

    loads[0].wait()
    send_first[:, 0] = by_channel(src_v[...])
    loads[1].wait()
    loads[2].wait()
    rates = decay_v[...]
    steps = (lax.broadcasted_iota(jnp.int32, (TILE, width), 0) + me * TILE).astype(F32)
    mod_v[...] = jnp.sqrt(2.0 * rates) * jnp.exp(-rates * steps)
    send_first[:, 1] = by_channel(filt_v[...].astype(F32) * mod_v[...])
    recv_first[me] = send_first[me]

    @pl.when(core == 0)
    def _():
        pl.semaphore_wait(barrier, n - 1)
        pl.semaphore_signal(all_in, inc=1, device_id={"seq": sibling}, device_id_type=MESH)

    @pl.when(core == 1)
    def _():
        pl.semaphore_wait(all_in, 1)

    def exchange(src, dst, sem, places):
        for offset in places:
            dest = index(offset)
            pltpu.make_async_remote_copy(
                src_ref=src.at[dest],
                dst_ref=dst.at[me],
                send_sem=send_sem.at[sem],
                recv_sem=recv_sem.at[sem],
                device_id={"seq": dest},
                device_id_type=MESH,
            ).start()

    def whole(src, dst, sem):
        return pltpu.make_async_remote_copy(
            src_ref=src.at[pl.ds(0, n - 1)],
            dst_ref=dst.at[pl.ds(0, n - 1)],
            send_sem=send_sem.at[sem],
            recv_sem=recv_sem.at[sem],
            device_id={"seq": index((0, 0, 1))},
            device_id_type=MESH,
        )

    exchange(send_first, recv_first, 0, offsets)

    loads[3].wait()
    for q in range(chunks):
        pipe_copy(q).wait_recv()
        chunk = xs[turns[q]]
        cols = pl.ds(pl.multiple_of(chunk * LANES, LANES), LANES)
        product = grad_v[:, cols].astype(F32) * gate_v[:, cols].astype(F32)
        send_grad[pl.ds(chunk * per_chunk, per_chunk)] = by_channel(product.astype(BF16))
        exchange(send_grad, recv_grad, 1, [o for o in offsets if o[0] == turns[q]])
    recv_grad[me] = send_grad[me]

    @pl.when(first)
    def _():
        pl.semaphore_wait(pipe_ready, 1)
        pass_on()

    def lines(block):
        return jnp.concatenate([block[:, j] for j in range(group)], axis=-1).reshape(rows, INNER)

    def forward(left, place):
        count = left.shape[0] // rows
        for at in (0, 512, 256, 768):
            result = jnp.dot(
                left, forward_v[0:INNER, at : at + 256], preferred_element_type=F32
            ) + jnp.dot(
                left, forward_v[INNER : 2 * INNER, at : at + 256], preferred_element_type=F32
            )
            for i in range(count):
                spec[place + i, :, at : at + 256] = result[i * rows : (i + 1) * rows]

    def multiply(kept, other, correlate, base):
        def step(g, carry):
            at = pl.multiple_of(g * LANES, LANES)
            real, imag = pl.ds(at, LANES), pl.ds(pl.multiple_of(at + INNER, LANES), LANES)
            lane = lax.broadcasted_iota(jnp.int32, (8, LANES), 1)
            sign = (1 - 2 * lax.rem(lane, 2)).astype(F32)
            for half in range(0, chans, 8):
                part = [pl.ds(b * chans + half, 8) for b in range(blocks)]
                raw = [(spec[kept, part[b], real], spec[kept, part[b], imag]) for b in range(blocks)]
                fold = [raw[0]]
                for b in range(1, blocks):
                    before = raw[b - 1]
                    fold.append((raw[b][0] - sign * before[1], raw[b][1] + sign * before[0]))
                right = [
                    (spec[other, part[b], real], spec[other, part[b], imag]) for b in range(blocks)
                ]
                for i in range(blocks):
                    total_r = total_i = None
                    for j in range(i, blocks) if correlate else range(i + 1):
                        kr, ki = fold[j - i] if correlate else fold[i - j]
                        br, bi = right[j]
                        if correlate:
                            term_r, term_i = kr * br + ki * bi, kr * bi - ki * br
                        else:
                            term_r, term_i = kr * br - ki * bi, kr * bi + ki * br
                        total_r = term_r if total_r is None else total_r + term_r
                        total_i = term_i if total_i is None else total_i + term_i
                    to = pl.ds(base + i * chans + half, 8)
                    prod[to, real] = total_r
                    prod[to, imag] = total_i
            return carry

        lax.fori_loop(0, INNER // LANES, step, 0, unroll=True)

    def inverse(count, store):
        left = prod[0 : count * rows].astype(BF16)
        half = 2 * INNER
        for at in range(0, INNER, 256):
            result = jnp.dot(
                left, inverse_v[0:half, at : at + 256], preferred_element_type=F32
            ) + jnp.dot(left, inverse_v[half : 2 * half, at : at + 256], preferred_element_type=F32)
            result = result.astype(BF16)
            for i in range(count):
                for j in range(256 // TILE):
                    piece = result[i * rows : (i + 1) * rows, j * TILE : (j + 1) * TILE]
                    piece = piece.reshape(blocks, chans, TILE)
                    for b in range(blocks):
                        store(i, b * group + at // TILE + j, piece[b])

    loads[4].wait()
    loads[5].wait()
    whole(send_first, recv_first, 0).wait_recv()
    block = recv_first[...].reshape(blocks, group, 2, chans, TILE)
    both = jnp.concatenate([lines(block[:, :, SOURCE]), lines(block[:, :, KERNEL])], axis=0)
    forward(both, SOURCE)
    multiply(KERNEL, SOURCE, False, 0)

    def store_conv(i, dest, piece):
        send_conv[dest] = piece

    inverse(1, store_conv)
    recv_conv[me] = send_conv[me]
    exchange(send_conv, recv_conv, 2, offsets)

    whole(send_grad, recv_grad, 1).wait_recv()
    forward(lines(recv_grad[...].reshape(blocks, group, chans, TILE)), GRAD)
    multiply(KERNEL, GRAD, True, 0)
    multiply(SOURCE, GRAD, True, rows)

    def store_pair(i, dest, piece):
        send_pair[dest, i] = piece

    inverse(2, store_pair)
    pair_v[me] = send_pair[me]
    exchange(send_pair, pair_v, 3, offsets)

    whole(send_conv, recv_conv, 2).wait_recv()
    turned = recv_conv[...].reshape(width, TILE).astype(F32).T
    og_v[...] = (grad_v[...].astype(F32) * turned).astype(BF16)

    for q in range(chunks):
        pipe_copy(q).wait_send()
    whole(send_first, recv_first, 0).wait_send()
    whole(send_grad, recv_grad, 1).wait_send()
    whole(send_conv, recv_conv, 2).wait_send()
    whole(send_pair, pair_v, 3).wait_send()
    whole(send_pair, pair_v, 3).wait_recv()


def finish(gate_v, pair_v, mod_v, out_gate, out_source, out_filter, source_v, filter_v, sems):
    width = mod_v.shape[1]
    chans = pair_v.shape[2]
    per_chunk = LANES // chans
    stores = []

    def store(src, dst):
        stores.append(pltpu.make_async_copy(src, dst, sems.at[len(stores)]))
        stores[-1].start()

    store(gate_v, out_gate.at[0])
    for q in range(width // LANES):
        cols = slice(q * LANES, (q + 1) * LANES)
        here = pair_v[q * per_chunk : (q + 1) * per_chunk]
        filter_v[:, cols] = here[:, 1].reshape(LANES, TILE).astype(F32).T * mod_v[:, cols]
        store(filter_v.at[:, cols], out_filter.at[0, :, cols])
        source_v[:, cols] = here[:, 0].reshape(LANES, TILE).astype(F32).T.astype(BF16)
        store(source_v.at[:, cols], out_source.at[0, :, cols])
    for started in stores:
        started.wait()


def local(n, nz, handoff, gate_input, source, long_filter, decay_rates):
    forward_table, inverse_table = tables()
    _, tokens, width = source.shape
    chans = width // n
    rows = n * TILE // INNER * chans
    block = (tokens, width)
    one, two = (n, chans, TILE), (n, 2, chans, TILE)
    hbm = lambda value: pltpu.with_memory_space_constraint(value, pltpu.HBM)
    results = pl.pallas_call(
        functools.partial(kernel, n, nz),
        out_shape=(pltpu.VMEM(block, BF16), pltpu.VMEM(two, BF16), pltpu.VMEM(block, F32)),
        in_specs=[pl.BlockSpec(memory_space=pltpu.HBM)] * 7,
        out_specs=[pl.BlockSpec(memory_space=pltpu.VMEM)] * 3,
        scratch_shapes=[
            pltpu.VMEM(block, BF16),
            pltpu.VMEM(block, BF16),
            pltpu.VMEM(block, BF16),
            pltpu.VMEM((1, width), F32),
            pltpu.VMEM(forward_table.shape, BF16),
            pltpu.VMEM(inverse_table.shape, BF16),
            pltpu.VMEM(block, BF16),
            pltpu.VMEM(two, BF16),
            pltpu.VMEM(two, BF16),
            pltpu.VMEM(one, BF16),
            pltpu.VMEM(one, BF16),
            pltpu.VMEM((3, rows, 2 * INNER), F32),
            pltpu.VMEM((2 * rows, 2 * INNER), F32),
            pltpu.VMEM(one, BF16),
            pltpu.VMEM(one, BF16),
            pltpu.VMEM(two, BF16),
            pltpu.SemaphoreType.DMA((6,)),
            pltpu.SemaphoreType.REGULAR,
            pltpu.SemaphoreType.REGULAR,
            pltpu.SemaphoreType.DMA((width // LANES,)),
            pltpu.SemaphoreType.DMA((width // LANES,)),
            pltpu.SemaphoreType.DMA((4,)),
            pltpu.SemaphoreType.DMA((4,)),
        ],
        compiler_params=pltpu.CompilerParams(
            collective_id=0, has_side_effects=True, vmem_limit_bytes=40 * 1024 * 1024
        ),
        cost_estimate=pl.CostEstimate(
            flops=2 * 6 * rows * 4 * INNER * INNER, bytes_accessed=6 << 20, transcendentals=0
        ),
    )(
        hbm(handoff),
        hbm(gate_input),
        hbm(source),
        hbm(long_filter),
        hbm(decay_rates),
        hbm(jnp.asarray(forward_table)),
        hbm(jnp.asarray(inverse_table)),
    )
    return pl.pallas_call(
        finish,
        out_shape=(
            jax.ShapeDtypeStruct(source.shape, BF16),
            jax.ShapeDtypeStruct(source.shape, BF16),
            jax.ShapeDtypeStruct(source.shape, F32),
        ),
        in_specs=[pl.BlockSpec(memory_space=pltpu.VMEM)] * 3,
        out_specs=[pl.BlockSpec(memory_space=pltpu.HBM)] * 3,
        scratch_shapes=[
            pltpu.VMEM(block, BF16),
            pltpu.VMEM(block, F32),
            pltpu.SemaphoreType.DMA((1 + 2 * (width // LANES),)),
        ],
        compiler_params=pltpu.CompilerParams(vmem_limit_bytes=4 * 1024 * 1024),
    )(*[pltpu.with_memory_space_constraint(r, pltpu.VMEM) for r in results])


def solution(mesh):
    tokens = P("pipe", "seq", None)
    return jax.shard_map(
        functools.partial(local, mesh.shape["seq"], mesh.shape["pipe"]),
        mesh=mesh,
        in_specs=(tokens, tokens, tokens, tokens, P("pipe", None)),
        out_specs=(tokens, tokens, tokens),
        check_vma=False,
    )
```

```python
import functools

import jax
import jax.numpy as jnp
import ml_dtypes
import numpy as np
from jax import lax
from jax.experimental import pallas as pl
from jax.experimental.pallas import tpu as pltpu
from jax.sharding import PartitionSpec as P

MESH = pl.DeviceIdType.MESH
F32, BF16 = jnp.float32, jnp.bfloat16
INNER = 512
TILE = 128
LANES = 128
SOURCE, KERNEL, GRAD = 0, 1, 2


def tables():
    token = np.arange(INNER, dtype=np.float64)[:, None]
    freq = np.arange(INNER, dtype=np.float64)[None, :] + 0.5
    angle = 2.0 * np.pi * ((token * freq) % (2 * INNER)) / (2 * INNER)
    forward = np.concatenate([np.cos(angle), -np.sin(angle)], axis=1)
    inverse = forward.T / INNER

    def split(table):
        high = table.astype(ml_dtypes.bfloat16)
        low = (table - high.astype(np.float64)).astype(ml_dtypes.bfloat16)
        return np.concatenate([high, low], axis=0)

    return split(forward), split(inverse)


def kernel(
    n,
    nz,
    handoff,
    gate,
    source,
    filt,
    decay,
    forward_hbm,
    inverse_hbm,
    og_v,
    pair_v,
    mod_v,
    src_v,
    gate_v,
    filt_v,
    decay_v,
    forward_v,
    inverse_v,
    grad_v,
    send_first,
    recv_first,
    send_grad,
    recv_grad,
    spec,
    prod,
    send_conv,
    recv_conv,
    send_pair,
    local_sem,
    pipe_ready,
    all_in,
    zero_in,
    pipe_send,
    pipe_recv,
    send_sem,
    recv_sem,
):
    me = lax.axis_index("seq")
    mz = lax.axis_index("pipe")
    above, below = lax.rem(mz + 1, nz), lax.rem(mz + nz - 1, nz)
    width = src_v.shape[1]
    chans = width // n
    chunks = width // LANES
    per_chunk = LANES // chans
    group = INNER // TILE
    blocks = n // group
    rows = blocks * chans

    nx, ny, nc = n // 8, 4, 2
    xs = [lax.rem(me // 8 + d, nx) for d in range(nx)]
    ys = [lax.rem(lax.rem(me // nc, ny) + d, ny) for d in range(ny)]
    cs = [lax.rem(lax.rem(me, nc) + d, nc) for d in range(nc)]

    def hops(offset):
        dx, dy, dc = offset
        return min(dx, nx - dx) + min(dy, ny - dy) + 0.1 * dc

    def index(offset):
        dx, dy, dc = offset
        return xs[dx] * (ny * nc) + ys[dy] * nc + cs[dc]

    offsets = [(dx, dy, dc) for dx in range(nx) for dy in range(ny) for dc in range(nc)]
    offsets = sorted(offsets, key=hops, reverse=True)[:-1]
    turns = sorted(range(nx), key=lambda d: min(d, nx - d), reverse=True)

    core = lax.rem(me, nc)
    second = me - core + 1
    sibling = me + 1 - 2 * core
    first, last = mz == 0, mz == nz - 1
    barrier = pltpu.get_barrier_semaphore()

    def greet(**place):
        pl.semaphore_signal(barrier, inc=1, device_id=place, device_id_type=MESH)

    @pl.when(first)
    def _():
        greet(pipe=above, seq=second)

        @pl.when(me == 0)
        def _():
            greet(seq=1)

        @pl.when(me != 0)
        def _():
            for offset in offsets:
                dest = index(offset)
                pl.when(dest != 1)(functools.partial(greet, seq=dest))

        greet(pipe=below, seq=second)

    @pl.when(jnp.logical_not(first))
    def _():
        @pl.when(jnp.logical_not(last))
        def _():
            greet(pipe=above, seq=second)

        greet(seq=sibling)
        for dx, dy, dc in offsets:
            if dc == 0:
                greet(seq=xs[dx] * (ny * nc) + ys[dy] * nc)

    loads = [
        pltpu.make_async_copy(source.at[0], src_v, local_sem.at[0]),
        pltpu.make_async_copy(filt.at[0], filt_v, local_sem.at[1]),
        pltpu.make_async_copy(decay, decay_v, local_sem.at[2]),
        pltpu.make_async_copy(gate.at[0], gate_v, local_sem.at[3]),
        pltpu.make_async_copy(forward_hbm, forward_v, local_sem.at[4]),
        pltpu.make_async_copy(inverse_hbm, inverse_v, local_sem.at[5]),
    ]
    for load in loads:
        load.start()

    def pipe_copy(q):
        at = pl.multiple_of(xs[turns[q]] * LANES, LANES)
        return pltpu.make_async_remote_copy(
            src_ref=handoff.at[0, :, pl.ds(at, LANES)],
            dst_ref=grad_v.at[:, pl.ds(at, LANES)],
            send_sem=pipe_send.at[q],
            recv_sem=pipe_recv.at[q],
            device_id={"pipe": below},
            device_id_type=MESH,
        )

    def pass_on():
        for q in range(chunks):
            pipe_copy(q).start()

    @pl.when(jnp.logical_and(core == 1, jnp.logical_not(first)))
    def _():
        pl.semaphore_wait(barrier, 3 + jnp.where(last, 2, 0))
        pl.semaphore_signal(pipe_ready, inc=1, device_id={"seq": sibling}, device_id_type=MESH)
        pass_on()

        @pl.when(last)
        def _():
            for to in (second - 1, second):
                pl.semaphore_signal(
                    pipe_ready, inc=1, device_id={"pipe": above, "seq": to}, device_id_type=MESH
                )

    @pl.when(jnp.logical_and(core == 0, jnp.logical_not(first)))
    def _():
        pl.semaphore_wait(pipe_ready, 1)
        pass_on()

    def by_channel(value):
        return value.astype(F32).T.astype(BF16).reshape(-1, chans, TILE)

    loads[0].wait()
    send_first[:, 0] = by_channel(src_v[...])
    loads[1].wait()
    loads[2].wait()
    rates = decay_v[...]
    steps = (lax.broadcasted_iota(jnp.int32, (TILE, width), 0) + me * TILE).astype(F32)
    mod_v[...] = jnp.sqrt(2.0 * rates) * jnp.exp(-rates * steps)
    send_first[:, 1] = by_channel(filt_v[...].astype(F32) * mod_v[...])
    recv_first[me] = send_first[me]

    @pl.when(jnp.logical_and(first, me != 1))
    def _():
        pl.semaphore_wait(barrier, n - 1 - jnp.where(me == 0, 0, 1))

        @pl.when(me == 2)
        def _():
            pl.semaphore_signal(all_in, inc=1, device_id={"seq": 1}, device_id_type=MESH)

    @pl.when(jnp.logical_and(core == 0, jnp.logical_not(first)))
    def _():
        pl.semaphore_wait(barrier, n - 1)

    @pl.when(jnp.logical_and(core == 0, jnp.logical_not(first)))
    def _():
        pl.semaphore_signal(all_in, inc=1, device_id={"seq": sibling}, device_id_type=MESH)

    @pl.when(jnp.logical_and(core == 1, jnp.logical_or(jnp.logical_not(first), me == 1)))
    def _():
        pl.semaphore_wait(all_in, 1)

    def send(src, dst, sem, dest):
        pltpu.make_async_remote_copy(
            src_ref=src.at[dest],
            dst_ref=dst.at[me],
            send_sem=send_sem.at[sem],
            recv_sem=recv_sem.at[sem],
            device_id={"seq": dest},
            device_id_type=MESH,
        ).start()

    def exchange(src, dst, sem, places):
        for offset in places:
            send(src, dst, sem, index(offset))

    def exchange_early(src, dst, sem, places):
        for offset in places:
            dest = index(offset)
            there = jnp.logical_or(jnp.logical_not(first), dest != 0)
            pl.when(there)(functools.partial(send, src, dst, sem, dest))

    def whole(src, dst, sem):
        return pltpu.make_async_remote_copy(
            src_ref=src.at[pl.ds(0, n - 1)],
            dst_ref=dst.at[pl.ds(0, n - 1)],
            send_sem=send_sem.at[sem],
            recv_sem=recv_sem.at[sem],
            device_id={"seq": index((0, 0, 1))},
            device_id_type=MESH,
        )

    exchange_early(send_first, recv_first, 0, offsets)

    @pl.when(jnp.logical_and(first, me == 1))
    def _():
        pl.semaphore_wait(barrier, 1)
        for offset in offsets:
            dest = index(offset)

            @pl.when(dest != 0)
            def _():
                pl.semaphore_signal(zero_in, inc=1, device_id={"seq": dest}, device_id_type=MESH)


    loads[3].wait()
    for q in range(chunks):
        pipe_copy(q).wait_recv()
        chunk = xs[turns[q]]
        cols = pl.ds(pl.multiple_of(chunk * LANES, LANES), LANES)
        product = grad_v[:, cols].astype(F32) * gate_v[:, cols].astype(F32)
        send_grad[pl.ds(chunk * per_chunk, per_chunk)] = by_channel(product.astype(BF16))
        exchange_early(send_grad, recv_grad, 1, [o for o in offsets if o[0] == turns[q]])
    recv_grad[me] = send_grad[me]

    @pl.when(jnp.logical_and(first, me != 0))
    def _():
        @pl.when(me != 1)
        def _():
            pl.semaphore_wait(zero_in, 1)

        send(send_first, recv_first, 0, 0)
        send(send_grad, recv_grad, 1, 0)

    @pl.when(first)
    def _():
        pl.semaphore_wait(pipe_ready, 1)
        pass_on()

    def lines(block):
        return jnp.concatenate([block[:, j] for j in range(group)], axis=-1).reshape(rows, INNER)

    def forward(left, place):
        count = left.shape[0] // rows
        for at in (0, 512, 256, 768):
            result = jnp.dot(
                left, forward_v[0:INNER, at : at + 256], preferred_element_type=F32
            ) + jnp.dot(
                left, forward_v[INNER : 2 * INNER, at : at + 256], preferred_element_type=F32
            )
            for i in range(count):
                spec[place + i, :, at : at + 256] = result[i * rows : (i + 1) * rows]

    def multiply(kept, other, correlate, base):
        def step(g, carry):
            at = pl.multiple_of(g * LANES, LANES)
            real, imag = pl.ds(at, LANES), pl.ds(pl.multiple_of(at + INNER, LANES), LANES)
            lane = lax.broadcasted_iota(jnp.int32, (8, LANES), 1)
            sign = (1 - 2 * lax.rem(lane, 2)).astype(F32)
            for half in range(0, chans, 8):
                part = [pl.ds(b * chans + half, 8) for b in range(blocks)]
                raw = [(spec[kept, part[b], real], spec[kept, part[b], imag]) for b in range(blocks)]
                fold = [raw[0]]
                for b in range(1, blocks):
                    before = raw[b - 1]
                    fold.append((raw[b][0] - sign * before[1], raw[b][1] + sign * before[0]))
                right = [
                    (spec[other, part[b], real], spec[other, part[b], imag]) for b in range(blocks)
                ]
                for i in range(blocks):
                    total_r = total_i = None
                    for j in range(i, blocks) if correlate else range(i + 1):
                        kr, ki = fold[j - i] if correlate else fold[i - j]
                        br, bi = right[j]
                        if correlate:
                            term_r, term_i = kr * br + ki * bi, kr * bi - ki * br
                        else:
                            term_r, term_i = kr * br - ki * bi, kr * bi + ki * br
                        total_r = term_r if total_r is None else total_r + term_r
                        total_i = term_i if total_i is None else total_i + term_i
                    to = pl.ds(base + i * chans + half, 8)
                    prod[to, real] = total_r
                    prod[to, imag] = total_i
            return carry

        lax.fori_loop(0, INNER // LANES, step, 0, unroll=True)

    def inverse(count, store):
        left = prod[0 : count * rows].astype(BF16)
        half = 2 * INNER
        for at in range(0, INNER, 256):
            result = jnp.dot(
                left, inverse_v[0:half, at : at + 256], preferred_element_type=F32
            ) + jnp.dot(left, inverse_v[half : 2 * half, at : at + 256], preferred_element_type=F32)
            result = result.astype(BF16)
            for i in range(count):
                for j in range(256 // TILE):
                    piece = result[i * rows : (i + 1) * rows, j * TILE : (j + 1) * TILE]
                    piece = piece.reshape(blocks, chans, TILE)
                    for b in range(blocks):
                        store(i, b * group + at // TILE + j, piece[b])

    loads[4].wait()
    loads[5].wait()
    whole(send_first, recv_first, 0).wait_recv()
    block = recv_first[...].reshape(blocks, group, 2, chans, TILE)
    both = jnp.concatenate([lines(block[:, :, SOURCE]), lines(block[:, :, KERNEL])], axis=0)
    forward(both, SOURCE)
    multiply(KERNEL, SOURCE, False, 0)

    def store_conv(i, dest, piece):
        send_conv[dest] = piece

    inverse(1, store_conv)
    recv_conv[me] = send_conv[me]
    exchange(send_conv, recv_conv, 2, offsets)

    whole(send_grad, recv_grad, 1).wait_recv()
    forward(lines(recv_grad[...].reshape(blocks, group, chans, TILE)), GRAD)
    multiply(KERNEL, GRAD, True, 0)
    multiply(SOURCE, GRAD, True, rows)

    def store_pair(i, dest, piece):
        send_pair[dest, i] = piece

    inverse(2, store_pair)
    pair_v[me] = send_pair[me]
    exchange(send_pair, pair_v, 3, offsets)

    whole(send_conv, recv_conv, 2).wait_recv()
    turned = recv_conv[...].reshape(width, TILE).astype(F32).T
    og_v[...] = (grad_v[...].astype(F32) * turned).astype(BF16)

    for q in range(chunks):
        pipe_copy(q).wait_send()
    whole(send_first, recv_first, 0).wait_send()
    whole(send_grad, recv_grad, 1).wait_send()
    whole(send_conv, recv_conv, 2).wait_send()
    whole(send_pair, pair_v, 3).wait_send()
    whole(send_pair, pair_v, 3).wait_recv()


def finish(gate_v, pair_v, mod_v, out_gate, out_source, out_filter, source_v, filter_v, sems):
    width = mod_v.shape[1]
    chans = pair_v.shape[2]
    per_chunk = LANES // chans
    stores = []

    def store(src, dst):
        stores.append(pltpu.make_async_copy(src, dst, sems.at[len(stores)]))
        stores[-1].start()

    store(gate_v, out_gate.at[0])
    for q in range(width // LANES):
        cols = slice(q * LANES, (q + 1) * LANES)
        here = pair_v[q * per_chunk : (q + 1) * per_chunk]
        filter_v[:, cols] = here[:, 1].reshape(LANES, TILE).astype(F32).T * mod_v[:, cols]
        store(filter_v.at[:, cols], out_filter.at[0, :, cols])
        source_v[:, cols] = here[:, 0].reshape(LANES, TILE).astype(F32).T.astype(BF16)
        store(source_v.at[:, cols], out_source.at[0, :, cols])
    for started in stores:
        started.wait()


def local(n, nz, handoff, gate_input, source, long_filter, decay_rates):
    forward_table, inverse_table = tables()
    _, tokens, width = source.shape
    chans = width // n
    rows = n * TILE // INNER * chans
    block = (tokens, width)
    one, two = (n, chans, TILE), (n, 2, chans, TILE)
    hbm = lambda value: pltpu.with_memory_space_constraint(value, pltpu.HBM)
    results = pl.pallas_call(
        functools.partial(kernel, n, nz),
        out_shape=(pltpu.VMEM(block, BF16), pltpu.VMEM(two, BF16), pltpu.VMEM(block, F32)),
        in_specs=[pl.BlockSpec(memory_space=pltpu.HBM)] * 7,
        out_specs=[pl.BlockSpec(memory_space=pltpu.VMEM)] * 3,
        scratch_shapes=[
            pltpu.VMEM(block, BF16),
            pltpu.VMEM(block, BF16),
            pltpu.VMEM(block, BF16),
            pltpu.VMEM((1, width), F32),
            pltpu.VMEM(forward_table.shape, BF16),
            pltpu.VMEM(inverse_table.shape, BF16),
            pltpu.VMEM(block, BF16),
            pltpu.VMEM(two, BF16),
            pltpu.VMEM(two, BF16),
            pltpu.VMEM(one, BF16),
            pltpu.VMEM(one, BF16),
            pltpu.VMEM((3, rows, 2 * INNER), F32),
            pltpu.VMEM((2 * rows, 2 * INNER), F32),
            pltpu.VMEM(one, BF16),
            pltpu.VMEM(one, BF16),
            pltpu.VMEM(two, BF16),
            pltpu.SemaphoreType.DMA((6,)),
            pltpu.SemaphoreType.REGULAR,
            pltpu.SemaphoreType.REGULAR,
            pltpu.SemaphoreType.REGULAR,
            pltpu.SemaphoreType.DMA((width // LANES,)),
            pltpu.SemaphoreType.DMA((width // LANES,)),
            pltpu.SemaphoreType.DMA((4,)),
            pltpu.SemaphoreType.DMA((4,)),
        ],
        compiler_params=pltpu.CompilerParams(
            collective_id=0, has_side_effects=True, vmem_limit_bytes=40 * 1024 * 1024
        ),
        cost_estimate=pl.CostEstimate(
            flops=2 * 6 * rows * 4 * INNER * INNER, bytes_accessed=6 << 20, transcendentals=0
        ),
    )(
        hbm(handoff),
        hbm(gate_input),
        hbm(source),
        hbm(long_filter),
        hbm(decay_rates),
        hbm(jnp.asarray(forward_table)),
        hbm(jnp.asarray(inverse_table)),
    )
    return pl.pallas_call(
        finish,
        out_shape=(
            jax.ShapeDtypeStruct(source.shape, BF16),
            jax.ShapeDtypeStruct(source.shape, BF16),
            jax.ShapeDtypeStruct(source.shape, F32),
        ),
        in_specs=[pl.BlockSpec(memory_space=pltpu.VMEM)] * 3,
        out_specs=[pl.BlockSpec(memory_space=pltpu.HBM)] * 3,
        scratch_shapes=[
            pltpu.VMEM(block, BF16),
            pltpu.VMEM(block, F32),
            pltpu.SemaphoreType.DMA((1 + 2 * (width // LANES),)),
        ],
        compiler_params=pltpu.CompilerParams(vmem_limit_bytes=4 * 1024 * 1024),
    )(*[pltpu.with_memory_space_constraint(r, pltpu.VMEM) for r in results])


def solution(mesh):
    tokens = P("pipe", "seq", None)
    return jax.shard_map(
        functools.partial(local, mesh.shape["seq"], mesh.shape["pipe"]),
        mesh=mesh,
        in_specs=(tokens, tokens, tokens, tokens, P("pipe", None)),
        out_specs=(tokens, tokens, tokens),
        check_vma=False,
    )
```

```python
import functools

import jax
import jax.numpy as jnp
import ml_dtypes
import numpy as np
from jax import lax
from jax.experimental import pallas as pl
from jax.experimental.pallas import tpu as pltpu
from jax.sharding import PartitionSpec as P

MESH = pl.DeviceIdType.MESH
F32, BF16 = jnp.float32, jnp.bfloat16
INNER = 512
TILE = 128
LANES = 128
SOURCE, KERNEL, GRAD = 0, 1, 2


def tables():
    token = np.arange(INNER, dtype=np.float64)[:, None]
    freq = np.arange(INNER, dtype=np.float64)[None, :] + 0.5
    angle = 2.0 * np.pi * ((token * freq) % (2 * INNER)) / (2 * INNER)
    forward = np.concatenate([np.cos(angle), -np.sin(angle)], axis=1)
    inverse = forward.T / INNER

    def split(table):
        high = table.astype(ml_dtypes.bfloat16)
        low = (table - high.astype(np.float64)).astype(ml_dtypes.bfloat16)
        return np.concatenate([high, low], axis=0)

    return split(forward), split(inverse)


def kernel(
    n,
    nz,
    handoff,
    gate,
    source,
    filt,
    decay,
    forward_hbm,
    inverse_hbm,
    og_v,
    pair_v,
    mod_v,
    src_v,
    gate_v,
    filt_v,
    decay_v,
    forward_v,
    inverse_v,
    grad_v,
    send_first,
    recv_first,
    send_grad,
    recv_grad,
    spec,
    prod,
    send_conv,
    recv_conv,
    send_pair,
    local_sem,
    pipe_ready,
    all_in,
    zero_in,
    pipe_send,
    pipe_recv,
    send_sem,
    recv_sem,
):
    me = lax.axis_index("seq")
    mz = lax.axis_index("pipe")
    above, below = lax.rem(mz + 1, nz), lax.rem(mz + nz - 1, nz)
    width = src_v.shape[1]
    chans = width // n
    chunks = width // LANES
    per_chunk = LANES // chans
    group = INNER // TILE
    blocks = n // group
    rows = blocks * chans

    nx, ny, nc = n // 8, 4, 2
    xs = [lax.rem(me // 8 + d, nx) for d in range(nx)]
    ys = [lax.rem(lax.rem(me // nc, ny) + d, ny) for d in range(ny)]
    cs = [lax.rem(lax.rem(me, nc) + d, nc) for d in range(nc)]

    def hops(offset):
        dx, dy, dc = offset
        return min(dx, nx - dx) + min(dy, ny - dy) + 0.1 * dc

    def index(offset):
        dx, dy, dc = offset
        return xs[dx] * (ny * nc) + ys[dy] * nc + cs[dc]

    offsets = [(dx, dy, dc) for dx in range(nx) for dy in range(ny) for dc in range(nc)]
    offsets = sorted(offsets, key=hops, reverse=True)[:-1]
    turns = sorted(range(nx), key=lambda d: min(d, nx - d), reverse=True)

    loads = [
        pltpu.make_async_copy(source.at[0], src_v, local_sem.at[0]),
        pltpu.make_async_copy(filt.at[0], filt_v, local_sem.at[1]),
        pltpu.make_async_copy(decay, decay_v, local_sem.at[2]),
        pltpu.make_async_copy(gate.at[0], gate_v, local_sem.at[3]),
        pltpu.make_async_copy(forward_hbm, forward_v, local_sem.at[4]),
        pltpu.make_async_copy(inverse_hbm, inverse_v, local_sem.at[5]),
    ]
    for load in loads:
        load.start()

    core = lax.rem(me, nc)
    second = me - core + 1
    sibling = me + 1 - 2 * core
    first, last = mz == 0, mz == nz - 1
    barrier = pltpu.get_barrier_semaphore()

    def greet(**place):
        pl.semaphore_signal(barrier, inc=1, device_id=place, device_id_type=MESH)

    @pl.when(first)
    def _():
        greet(pipe=above, seq=second)

        @pl.when(me == 0)
        def _():
            greet(seq=1)

        @pl.when(me != 0)
        def _():
            for offset in offsets:
                dest = index(offset)
                pl.when(dest != 1)(functools.partial(greet, seq=dest))

        greet(pipe=below, seq=second)

    @pl.when(jnp.logical_not(first))
    def _():
        @pl.when(jnp.logical_not(last))
        def _():
            greet(pipe=above, seq=second)

        greet(seq=sibling)
        for dx, dy, dc in offsets:
            if dc == 0:
                greet(seq=xs[dx] * (ny * nc) + ys[dy] * nc)

    def pipe_copy(q):
        at = pl.multiple_of(xs[turns[q]] * LANES, LANES)
        return pltpu.make_async_remote_copy(
            src_ref=handoff.at[0, :, pl.ds(at, LANES)],
            dst_ref=grad_v.at[:, pl.ds(at, LANES)],
            send_sem=pipe_send.at[q],
            recv_sem=pipe_recv.at[q],
            device_id={"pipe": below},
            device_id_type=MESH,
        )

    def pass_on():
        for q in range(chunks):
            pipe_copy(q).start()

    @pl.when(jnp.logical_and(core == 1, jnp.logical_not(first)))
    def _():
        pl.semaphore_wait(barrier, 3 + jnp.where(last, 2, 0))
        pl.semaphore_signal(pipe_ready, inc=1, device_id={"seq": sibling}, device_id_type=MESH)
        pass_on()

        @pl.when(last)
        def _():
            for to in (second - 1, second):
                pl.semaphore_signal(
                    pipe_ready, inc=1, device_id={"pipe": above, "seq": to}, device_id_type=MESH
                )

    @pl.when(jnp.logical_and(core == 0, jnp.logical_not(first)))
    def _():
        pl.semaphore_wait(pipe_ready, 1)
        pass_on()

    def by_channel(value):
        return value.astype(F32).T.astype(BF16).reshape(-1, chans, TILE)

    loads[0].wait()
    send_first[:, 0] = by_channel(src_v[...])
    loads[1].wait()
    loads[2].wait()
    rates = decay_v[...]
    steps = (lax.broadcasted_iota(jnp.int32, (TILE, width), 0) + me * TILE).astype(F32)
    mod_v[...] = jnp.sqrt(2.0 * rates) * jnp.exp(-rates * steps)
    send_first[:, 1] = by_channel(filt_v[...].astype(F32) * mod_v[...])
    recv_first[me] = send_first[me]

    @pl.when(jnp.logical_and(first, me != 1))
    def _():
        pl.semaphore_wait(barrier, n - 1 - jnp.where(me == 0, 0, 1))

        @pl.when(me == 2)
        def _():
            pl.semaphore_signal(all_in, inc=1, device_id={"seq": 1}, device_id_type=MESH)

    @pl.when(jnp.logical_and(core == 0, jnp.logical_not(first)))
    def _():
        pl.semaphore_wait(barrier, n - 1)

    @pl.when(jnp.logical_and(core == 0, jnp.logical_not(first)))
    def _():
        pl.semaphore_signal(all_in, inc=1, device_id={"seq": sibling}, device_id_type=MESH)

    @pl.when(jnp.logical_and(core == 1, jnp.logical_or(jnp.logical_not(first), me == 1)))
    def _():
        pl.semaphore_wait(all_in, 1)

    def send(src, dst, sem, dest):
        pltpu.make_async_remote_copy(
            src_ref=src.at[dest],
            dst_ref=dst.at[me],
            send_sem=send_sem.at[sem],
            recv_sem=recv_sem.at[sem],
            device_id={"seq": dest},
            device_id_type=MESH,
        ).start()

    def exchange(src, dst, sem, places):
        for offset in places:
            send(src, dst, sem, index(offset))

    def exchange_early(src, dst, sem, places):
        for offset in places:
            dest = index(offset)
            there = jnp.logical_or(jnp.logical_not(first), dest != 0)
            pl.when(there)(functools.partial(send, src, dst, sem, dest))

    def whole(src, dst, sem):
        return pltpu.make_async_remote_copy(
            src_ref=src.at[pl.ds(0, n - 1)],
            dst_ref=dst.at[pl.ds(0, n - 1)],
            send_sem=send_sem.at[sem],
            recv_sem=recv_sem.at[sem],
            device_id={"seq": index((0, 0, 1))},
            device_id_type=MESH,
        )

    exchange_early(send_first, recv_first, 0, offsets)

    @pl.when(jnp.logical_and(first, me == 1))
    def _():
        pl.semaphore_wait(barrier, 1)
        for offset in offsets:
            dest = index(offset)

            @pl.when(dest != 0)
            def _():
                pl.semaphore_signal(zero_in, inc=1, device_id={"seq": dest}, device_id_type=MESH)


    loads[3].wait()
    for q in range(chunks):
        pipe_copy(q).wait_recv()
        chunk = xs[turns[q]]
        cols = pl.ds(pl.multiple_of(chunk * LANES, LANES), LANES)
        product = grad_v[:, cols].astype(F32) * gate_v[:, cols].astype(F32)
        send_grad[pl.ds(chunk * per_chunk, per_chunk)] = by_channel(product.astype(BF16))
        exchange_early(send_grad, recv_grad, 1, [o for o in offsets if o[0] == turns[q]])
    recv_grad[me] = send_grad[me]

    @pl.when(jnp.logical_and(first, me != 0))
    def _():
        @pl.when(me != 1)
        def _():
            pl.semaphore_wait(zero_in, 1)

        send(send_first, recv_first, 0, 0)
        send(send_grad, recv_grad, 1, 0)

    @pl.when(first)
    def _():
        pl.semaphore_wait(pipe_ready, 1)
        pass_on()

    def lines(block):
        return jnp.concatenate([block[:, j] for j in range(group)], axis=-1).reshape(rows, INNER)

    def forward(left, place):
        count = left.shape[0] // rows
        for at in (0, 512, 256, 768):
            result = jnp.dot(
                left, forward_v[0:INNER, at : at + 256], preferred_element_type=F32
            ) + jnp.dot(
                left, forward_v[INNER : 2 * INNER, at : at + 256], preferred_element_type=F32
            )
            for i in range(count):
                spec[place + i, :, at : at + 256] = result[i * rows : (i + 1) * rows]

    def multiply(kept, other, correlate, base):
        def step(g, carry):
            at = pl.multiple_of(g * LANES, LANES)
            real, imag = pl.ds(at, LANES), pl.ds(pl.multiple_of(at + INNER, LANES), LANES)
            lane = lax.broadcasted_iota(jnp.int32, (8, LANES), 1)
            sign = (1 - 2 * lax.rem(lane, 2)).astype(F32)
            for half in range(0, chans, 8):
                part = [pl.ds(b * chans + half, 8) for b in range(blocks)]
                raw = [(spec[kept, part[b], real], spec[kept, part[b], imag]) for b in range(blocks)]
                fold = [raw[0]]
                for b in range(1, blocks):
                    before = raw[b - 1]
                    fold.append((raw[b][0] - sign * before[1], raw[b][1] + sign * before[0]))
                right = [
                    (spec[other, part[b], real], spec[other, part[b], imag]) for b in range(blocks)
                ]
                mixed = [kr - ki if correlate else kr + ki for kr, ki in fold]
                sums = [br + bi for br, bi in right]
                for i in range(blocks):
                    real_sum = imag_sum = mixed_sum = None
                    for j in range(i, blocks) if correlate else range(i + 1):
                        d = j - i if correlate else i - j
                        reals, imags = fold[d][0] * right[j][0], fold[d][1] * right[j][1]
                        mixes = mixed[d] * sums[j]
                        real_sum = reals if real_sum is None else real_sum + reals
                        imag_sum = imags if imag_sum is None else imag_sum + imags
                        mixed_sum = mixes if mixed_sum is None else mixed_sum + mixes
                    if correlate:
                        total_r, total_i = real_sum + imag_sum, mixed_sum - real_sum + imag_sum
                    else:
                        total_r, total_i = real_sum - imag_sum, mixed_sum - real_sum - imag_sum
                    to = pl.ds(base + i * chans + half, 8)
                    prod[to, real] = total_r
                    prod[to, imag] = total_i
            return carry

        lax.fori_loop(0, INNER // LANES, step, 0, unroll=True)

    def inverse(count, store):
        left = prod[0 : count * rows].astype(BF16)
        half = 2 * INNER
        for at in range(0, INNER, 256):
            result = jnp.dot(
                left, inverse_v[0:half, at : at + 256], preferred_element_type=F32
            ) + jnp.dot(left, inverse_v[half : 2 * half, at : at + 256], preferred_element_type=F32)
            result = result.astype(BF16)
            for i in range(count):
                for j in range(256 // TILE):
                    piece = result[i * rows : (i + 1) * rows, j * TILE : (j + 1) * TILE]
                    piece = piece.reshape(blocks, chans, TILE)
                    for b in range(blocks):
                        store(i, b * group + at // TILE + j, piece[b])

    loads[4].wait()
    loads[5].wait()
    whole(send_first, recv_first, 0).wait_recv()
    block = recv_first[...].reshape(blocks, group, 2, chans, TILE)
    both = jnp.concatenate([lines(block[:, :, SOURCE]), lines(block[:, :, KERNEL])], axis=0)
    forward(both, SOURCE)
    multiply(KERNEL, SOURCE, False, 0)

    def store_conv(i, dest, piece):
        send_conv[dest] = piece

    inverse(1, store_conv)
    recv_conv[me] = send_conv[me]
    exchange(send_conv, recv_conv, 2, offsets)

    whole(send_grad, recv_grad, 1).wait_recv()
    forward(lines(recv_grad[...].reshape(blocks, group, chans, TILE)), GRAD)
    multiply(KERNEL, GRAD, True, 0)
    multiply(SOURCE, GRAD, True, rows)

    def store_pair(i, dest, piece):
        send_pair[dest, i] = piece

    inverse(2, store_pair)
    pair_v[me] = send_pair[me]
    exchange(send_pair, pair_v, 3, offsets)

    whole(send_conv, recv_conv, 2).wait_recv()
    turned = recv_conv[...].reshape(width, TILE).astype(F32).T
    og_v[...] = (grad_v[...].astype(F32) * turned).astype(BF16)

    for q in range(chunks):
        pipe_copy(q).wait_send()
    whole(send_first, recv_first, 0).wait_send()
    whole(send_grad, recv_grad, 1).wait_send()
    whole(send_conv, recv_conv, 2).wait_send()
    whole(send_pair, pair_v, 3).wait_send()
    whole(send_pair, pair_v, 3).wait_recv()


def finish(gate_v, pair_v, mod_v, out_gate, out_source, out_filter, source_v, filter_v, sems):
    width = mod_v.shape[1]
    chans = pair_v.shape[2]
    per_chunk = LANES // chans
    stores = []

    def store(src, dst):
        stores.append(pltpu.make_async_copy(src, dst, sems.at[len(stores)]))
        stores[-1].start()

    store(gate_v, out_gate.at[0])
    for q in range(width // LANES):
        cols = slice(q * LANES, (q + 1) * LANES)
        here = pair_v[q * per_chunk : (q + 1) * per_chunk]
        filter_v[:, cols] = here[:, 1].reshape(LANES, TILE).astype(F32).T * mod_v[:, cols]
        store(filter_v.at[:, cols], out_filter.at[0, :, cols])
        source_v[:, cols] = here[:, 0].reshape(LANES, TILE).astype(F32).T.astype(BF16)
        store(source_v.at[:, cols], out_source.at[0, :, cols])
    for started in stores:
        started.wait()


def local(n, nz, handoff, gate_input, source, long_filter, decay_rates):
    forward_table, inverse_table = tables()
    _, tokens, width = source.shape
    chans = width // n
    rows = n * TILE // INNER * chans
    block = (tokens, width)
    one, two = (n, chans, TILE), (n, 2, chans, TILE)
    hbm = lambda value: pltpu.with_memory_space_constraint(value, pltpu.HBM)
    results = pl.pallas_call(
        functools.partial(kernel, n, nz),
        out_shape=(pltpu.VMEM(block, BF16), pltpu.VMEM(two, BF16), pltpu.VMEM(block, F32)),
        in_specs=[pl.BlockSpec(memory_space=pltpu.HBM)] * 7,
        out_specs=[pl.BlockSpec(memory_space=pltpu.VMEM)] * 3,
        scratch_shapes=[
            pltpu.VMEM(block, BF16),
            pltpu.VMEM(block, BF16),
            pltpu.VMEM(block, BF16),
            pltpu.VMEM((1, width), F32),
            pltpu.VMEM(forward_table.shape, BF16),
            pltpu.VMEM(inverse_table.shape, BF16),
            pltpu.VMEM(block, BF16),
            pltpu.VMEM(two, BF16),
            pltpu.VMEM(two, BF16),
            pltpu.VMEM(one, BF16),
            pltpu.VMEM(one, BF16),
            pltpu.VMEM((3, rows, 2 * INNER), F32),
            pltpu.VMEM((2 * rows, 2 * INNER), F32),
            pltpu.VMEM(one, BF16),
            pltpu.VMEM(one, BF16),
            pltpu.VMEM(two, BF16),
            pltpu.SemaphoreType.DMA((6,)),
            pltpu.SemaphoreType.REGULAR,
            pltpu.SemaphoreType.REGULAR,
            pltpu.SemaphoreType.REGULAR,
            pltpu.SemaphoreType.DMA((width // LANES,)),
            pltpu.SemaphoreType.DMA((width // LANES,)),
            pltpu.SemaphoreType.DMA((4,)),
            pltpu.SemaphoreType.DMA((4,)),
        ],
        compiler_params=pltpu.CompilerParams(
            collective_id=0, has_side_effects=True, vmem_limit_bytes=40 * 1024 * 1024
        ),
        cost_estimate=pl.CostEstimate(
            flops=2 * 6 * rows * 4 * INNER * INNER, bytes_accessed=6 << 20, transcendentals=0
        ),
    )(
        hbm(handoff),
        hbm(gate_input),
        hbm(source),
        hbm(long_filter),
        hbm(decay_rates),
        hbm(jnp.asarray(forward_table)),
        hbm(jnp.asarray(inverse_table)),
    )
    return pl.pallas_call(
        finish,
        out_shape=(
            jax.ShapeDtypeStruct(source.shape, BF16),
            jax.ShapeDtypeStruct(source.shape, BF16),
            jax.ShapeDtypeStruct(source.shape, F32),
        ),
        in_specs=[pl.BlockSpec(memory_space=pltpu.VMEM)] * 3,
        out_specs=[pl.BlockSpec(memory_space=pltpu.HBM)] * 3,
        scratch_shapes=[
            pltpu.VMEM(block, BF16),
            pltpu.VMEM(block, F32),
            pltpu.SemaphoreType.DMA((1 + 2 * (width // LANES),)),
        ],
        compiler_params=pltpu.CompilerParams(vmem_limit_bytes=4 * 1024 * 1024),
    )(*[pltpu.with_memory_space_constraint(r, pltpu.VMEM) for r in results])


def solution(mesh):
    tokens = P("pipe", "seq", None)
    return jax.shard_map(
        functools.partial(local, mesh.shape["seq"], mesh.shape["pipe"]),
        mesh=mesh,
        in_specs=(tokens, tokens, tokens, tokens, P("pipe", None)),
        out_specs=(tokens, tokens, tokens),
        check_vma=False,
    )
```
